32 devices in a mesh: dp: 16 (over z, y, x), tensor: 2 (over core).
Axes of the slice: x: 2, y: 2, z: 4, core: 2. Of those that a mesh axis runs over, the one named last changes fastest.
Arguments:
- tokens: bfloat16 [2048, 768], P('dp'), may hold values from -6 to 6
- gain_first: float32 [768], replicated, may hold values from 0.5 to 1.5
- shift_first: float32 [768], replicated, may hold values from -1.5 to 1.5
- qkv_weight: bfloat16 [768, 3, 768], P(None, None, 'tensor'), may hold values from -0.21875 to 0.21875
- qv_bias: float32 [2, 768], P(None, 'tensor'), may hold values from -2.5 to 2.5
- out_weight: bfloat16 [768, 768], P('tensor'), may hold values from -0.875 to 0.875
- out_bias: float32 [768], replicated, may hold values from -1.5 to 1.5
- gain_second: float32 [768], replicated, may hold values from 0.5 to 1.5
- shift_second: float32 [768], replicated, may hold values from -1.5 to 1.5
- up_weight: bfloat16 [768, 3072], P(None, 'tensor'), may hold values from -0.21875 to 0.21875
- up_bias: float32 [3072], P('tensor'), may hold values from -1.5 to 1.5
- down_weight: bfloat16 [3072, 768], P('tensor'), may hold values from -0.109375 to 0.109375
- down_bias: float32 [768], replicated, may hold values from -1.5 to 1.5
- doc_lengths: int32 [64], P('dp'), may hold values from 0 to 128, as said below
- upstream: bfloat16 [2048, 768], P('dp'), may hold values from -6 to 6
Outputs:
- layer_out: bfloat16 [2048, 768], P('dp')
- grad_tokens: bfloat16 [2048, 768], P('dp')
- grad_gain_first: float32 [768], replicated
- grad_shift_first: float32 [768], replicated
- grad_qkv_weight: float32 [768, 3, 768], P('dp', None, 'tensor')
- grad_qv_bias: float32 [2, 768], P(None, 'tensor')
- grad_out_weight: float32 [768, 768], P('tensor', 'dp')
- grad_out_bias: float32 [768], replicated
- grad_gain_second: float32 [768], replicated
- grad_shift_second: float32 [768], replicated
- grad_up_weight: float32 [768, 3072], P('dp', 'tensor')
- grad_up_bias: float32 [3072], P('tensor')
- grad_down_weight: float32 [3072, 768], P('tensor', 'dp')
- grad_down_bias: float32 [768], replicated
The draws below stay inside these ranges and needn't reach their ends.
Inputs may be any that keep to these rules, and one draw needn't show every extreme that they name: `doc_lengths`: on each index of dp the 4 lengths sum to 128 or less; on one index a single sequence fills all 128 slots.
All inputs are finite; a program needn't handle non-finite values.
Results may differ from the reference program's by a relative error of at most 0.011.
Values sent between devices are 32-bit elements; how exact they have to be, the bound alone decides.
No kernel may reach another device: no remote copies, remote signals or barrier semaphores. Data moves between devices by JAX's collectives and lax.ppermute only.
A program may use at most 128 MiB of HBM per device.

```python
import jax
import jax.numpy as jnp
from jax import lax

D = 768
HEADS = 12
HD = 64
FF = 3072
CAP = 128
SLOTS = 4
TOKENS = 2048
SLOTS_ALL = 64
N_DP = 16


def draw_doc_lengths(key, part):
    key = jax.random.fold_in(key, 11)
    first_key, second_key, third_key = jax.random.split(key, 3)
    devices_all = SLOTS_ALL // SLOTS
    totals = jax.random.randint(first_key, (devices_all,), CAP // 4, CAP + 1).astype(jnp.int32)
    full_row = jax.random.randint(second_key, (), 0, devices_all)
    row_ids = jnp.arange(devices_all, dtype=jnp.int32)
    totals = jnp.where(row_ids == full_row, CAP, totals).astype(jnp.int32)
    cuts = jax.random.randint(third_key, (devices_all, SLOTS - 1), 0, CAP + 1).astype(jnp.int32)
    cuts = jnp.sort(jnp.minimum(cuts, totals[:, None]), axis=1)
    edges = jnp.concatenate([jnp.zeros((devices_all, 1), jnp.int32), cuts, totals[:, None]], 1)
    lengths = edges[:, 1:] - edges[:, :-1]
    single = jnp.concatenate([jnp.full((devices_all, 1), CAP, jnp.int32), jnp.zeros((devices_all, SLOTS - 1), jnp.int32)], 1)
    lengths = jnp.where((row_ids == full_row)[:, None], single, lengths)
    return lengths.reshape(-1).astype(jnp.int32)


def with_spikes(result, stream_key, source, target, shards_of, factor):
    def block_of(position):
        return (jnp.arange(result.shape[position]) // (result.shape[position] // shards_of)).reshape((-1,) + (1,) * (result.ndim - 1 - position))

    one_side = jax.random.permutation(stream_key, shards_of)[block_of(target)]
    second = (block_of(target) + shards_of // 2) % shards_of
    return jnp.where((block_of(source) == one_side) | (block_of(source) == second), factor * result, result)


def steps_of(own_key, dims, pieces, smallest, high):
    factor_of = 1.0
    for axis_at, blocks in pieces:
        draws = jax.random.uniform(jax.random.fold_in(jax.random.fold_in(own_key, 6), axis_at), (blocks,), jnp.float32, smallest / len(pieces), high / len(pieces))
        factor_of = factor_of * jnp.repeat(jnp.exp(draws), dims[axis_at] // blocks).reshape((-1,) + (1,) * (len(dims) - 1 - axis_at))
    return factor_of


def noise(own_key, dims, scale, bound, pieces=(), kind=jnp.bfloat16):
    entries = jax.random.normal(own_key, dims, jnp.float32) * scale
    if len(pieces) > 0:
        entries = steps_of(own_key, dims, pieces, -0.22, 0.18) * entries
    return jnp.clip(entries, min=-bound, max=bound).astype(kind)


def gaussian_with(rng, dims, deviation, most, cuts, heavy, kind=jnp.bfloat16):
    drawn = deviation * jax.random.normal(rng, dims, jnp.float32)
    if cuts:
        drawn = drawn * steps_of(rng, dims, cuts, -0.22, 0.18)
    return jnp.clip(with_spikes(drawn, jax.random.fold_in(rng, 3), *heavy), -most, most).astype(kind)


def setup_inputs(seed: int = 0) -> dict:
    key_of = jax.random.split(jax.random.key(seed), 16)
    return {
        "tokens": gaussian_with(key_of[0], (TOKENS, D), 1.0, 6.0, ((0, 16),), (0, 1, 16, 2.0)),
        "gain_first": jnp.clip(1.0 + 0.1 * jax.random.normal(key_of[1], (D,), jnp.float32), 0.5, 1.5),
        "shift_first": noise(key_of[2], (D,), 0.3, 1.5, (), jnp.float32),
        "qkv_weight": noise(key_of[3], (D, 3, D), D ** -0.5, 0.21875, ((2, 2),)),
        "qv_bias": noise(key_of[4], (2, D), 0.5, 2.5, ((1, 2),), jnp.float32),
        "out_weight": noise(key_of[5], (D, D), (D // 16) ** -0.5, 0.875, ((0, 2),)),
        "out_bias": noise(key_of[6], (D,), 0.3, 1.5, (), jnp.float32),
        "gain_second": jnp.clip(1.0 + 0.1 * jax.random.normal(key_of[7], (D,), jnp.float32), 0.5, 1.5),
        "shift_second": noise(key_of[8], (D,), 0.3, 1.5, (), jnp.float32),
        "up_weight": noise(key_of[9], (D, FF), D ** -0.5, 0.21875, ((1, 2),)),
        "up_bias": noise(key_of[10], (FF,), 0.3, 1.5, ((0, 2),), jnp.float32),
        "down_weight": noise(key_of[11], (FF, D), FF ** -0.5, 0.109375, ((0, 2),)),
        "down_bias": noise(key_of[12], (D,), 0.3, 1.5, (), jnp.float32),
        "doc_lengths": draw_doc_lengths(jax.random.fold_in(key_of[15], 71), 0),
        "upstream": gaussian_with(key_of[14], (TOKENS, D), 1.0, 6.0, ((0, 16),), (0, 1, 16, 2.0)),
    }


@jax.custom_vjp
def low(v):
    return lax.optimization_barrier(v.astype(jnp.bfloat16)).astype(jnp.float32)

@jax.custom_vjp
def low_back(v):
    return v

def low_keep(v):
    return (low(v), None)

def low_pass(kept, grad):
    return (grad,)

def back_keep(v):
    return (v, None)

def back_low(kept, grad):
    return (low(grad),)
low.defvjp(low_keep, low_pass)
low_back.defvjp(back_keep, back_low)
epsilon = 1e-05
highest = lax.Precision.HIGHEST

def layer_norm(values, scales, offset):
    average = lax.optimization_barrier(jnp.mean(values, -1, keepdims=True))
    centred = values - average
    spread = lax.optimization_barrier(jnp.mean(centred * centred, -1, keepdims=True))
    return centred * lax.rsqrt(spread + epsilon) * scales + offset

def doc_layout(doc_lengths):
    per_device = doc_lengths.reshape(N_DP, SLOTS)
    doc_ends = jnp.cumsum(per_device, axis=1).astype(jnp.int32)
    offsets = jnp.arange(CAP, dtype=jnp.int32)
    segment = lax.optimization_barrier(jnp.sum((offsets[None, :, None] >= doc_ends[:, None, :]).astype(jnp.int32), -1))
    filled = offsets[None, :] < doc_ends[:, -1:]
    return (segment, filled)

def attend(block_data):
    queries, keys_here, values_here, segment, filled = block_data
    offsets = jnp.arange(CAP, dtype=jnp.int32)
    visible = (segment[:, None] == segment[None, :]) & (offsets[None, :] <= offsets[:, None]) & filled[None, :]
    visible = visible | (offsets[:, None] == offsets[None, :])
    scores = jnp.einsum('qhd,khd->hqk', queries, keys_here, precision=highest) * HD ** (-0.5)
    scores = low_back(scores)
    scores = jnp.where(visible[None], scores, -1e+30)
    highest_score = lax.optimization_barrier(jnp.max(scores, -1, keepdims=True))
    weights = jnp.exp(scores - highest_score)
    probs = low(weights / lax.optimization_barrier(jnp.sum(weights, -1, keepdims=True)))
    return jnp.einsum('hqk,khd->qhd', probs, values_here, precision=highest)

def forward(tokens, gain_first, shift_first, qkv_weight, qv_bias, out_weight, out_bias, gain_second, shift_second, up_weight, up_bias, down_weight, down_bias, segment, filled):
    normed = low(layer_norm(tokens, gain_first, shift_first))
    projected = jnp.einsum('td,dcf->tcf', normed, qkv_weight, precision=highest)
    qkv_shift = jnp.stack([qv_bias[0], jnp.zeros_like(qv_bias[0]), qv_bias[1]])
    projected = low(low_back(projected + qkv_shift)).reshape(N_DP, CAP, 3, HEADS, HD)
    attended = lax.map(jax.checkpoint(attend), (projected[:, :, 0], projected[:, :, 1], projected[:, :, 2], segment, filled))
    attended = low(low_back(attended.reshape(TOKENS, D)))
    after_attn = tokens + low_back(jnp.dot(attended, out_weight, precision=highest)) + out_bias
    mlp_in = low(layer_norm(after_attn, gain_second, shift_second))
    hidden = low_back(jnp.dot(mlp_in, up_weight, precision=highest) + up_bias)
    active = low(jax.nn.gelu(hidden, approximate=True))
    return after_attn + jnp.dot(active, down_weight, precision=highest) + down_bias

def reference(tokens, gain_first, shift_first, qkv_weight, qv_bias, out_weight, out_bias, gain_second, shift_second, up_weight, up_bias, down_weight, down_bias, doc_lengths, upstream):
    segment, filled = doc_layout(doc_lengths)
    inputs = [arr.astype(jnp.float32) for arr in (tokens, gain_first, shift_first, qkv_weight, qv_bias, out_weight, out_bias, gain_second, shift_second, up_weight, up_bias, down_weight, down_bias)]
    cotangent = upstream.astype(jnp.float32) * filled.reshape(TOKENS, 1).astype(jnp.float32)
    layer_out, pullback = jax.vjp(lambda *params: forward(*params, segment, filled), *inputs)
    grads = pullback(cotangent)
    return (layer_out.astype(jnp.bfloat16), grads[0].astype(jnp.bfloat16), grads[1], grads[2], grads[3], grads[4], grads[5], grads[6], grads[7], grads[8], grads[9], grads[10], grads[11], grads[12])
```

```python
import functools

import jax
import jax.numpy as jnp
from jax import lax
from jax.experimental import pallas as pl
from jax.experimental.pallas import tpu as pltpu
from jax.sharding import PartitionSpec as P

HD = 64
PAIR = 128
GROUP = 4
SLOTS = 4
EPS = 1e-05
F32 = jnp.float32
BF16 = jnp.bfloat16
SCALE = 1.0
COPY1 = 20.0
COPY2 = 20.0
ATTB = 0.05
MIDU = 20.0
ATT = 2.2
MLPF = 1.8
BACK = 0.05
TOKEN_VMEM = 60 * 1024 * 1024
VMEM_BYTES = 16 * 1024 * 1024


def dot(a, b):
    return lax.dot_general(a, b, (((1,), (0,)), ((), ())), preferred_element_type=F32)


def dot_bt(a, b):
    return lax.dot_general(a, b, (((1,), (1,)), ((), ())), preferred_element_type=F32)


def dot_at(a, b):
    return lax.dot_general(a, b, (((0,), (0,)), ((), ())), preferred_element_type=F32)


def normalize(x):
    centred = x - jnp.mean(x, -1, keepdims=True)
    spread = jnp.mean(centred * centred, -1, keepdims=True)
    scale = lax.rsqrt(spread + EPS)
    return centred * scale, scale


def normalize_back(grad, normal, scale):
    return scale * (
        grad
        - jnp.mean(grad, -1, keepdims=True)
        - normal * jnp.mean(grad * normal, -1, keepdims=True)
    )


def own_rows(width, n_dp):
    parts = n_dp // GROUP
    place = lax.axis_index("dp")
    group, rest = place // parts, place % parts
    share = width // GROUP
    if parts != 4:
        row = lax.broadcasted_iota(jnp.int32, (share, width), 0)
        column = lax.broadcasted_iota(jnp.int32, (share, width), 1)
        return (column - row == group * share).astype(F32).astype(BF16)
    piece = share // parts
    row = lax.broadcasted_iota(jnp.int32, (piece, width), 0)
    column = lax.broadcasted_iota(jnp.int32, (piece, width), 1)
    picks = []
    for k in range(parts):
        base = group * share + jnp.bitwise_xor(rest, k) * piece
        picks.append((column - row == base).astype(F32))
    return jnp.concatenate(picks, 0).astype(BF16)


def fetch(pairs, sems):
    copies = [pltpu.make_async_copy(a, b, sems.at[i]) for i, (a, b) in enumerate(pairs)]
    for copy in copies:
        copy.start()
    for copy in copies:
        copy.wait()


def token_message_kernel(
    tokens_hbm, doc_hbm, message, other, zeros, tokens, doc_lengths, sems
):
    fetch(
        [
            (tokens_hbm, tokens),
            (doc_hbm, doc_lengths),
        ],
        sems,
    )
    zeros[...] = jnp.zeros_like(zeros)
    rows, width = tokens.shape
    half = rows // 2
    core = lax.axis_index("tensor")
    here = pl.multiple_of(core * half, half)
    there = pl.multiple_of((1 - core) * half, half)
    for at in range(0, width, PAIR):
        to = at // PAIR * half
        message[to : to + half, :] = tokens[pl.ds(here, half), at : at + PAIR].astype(F32)
        other[to : to + half, :] = tokens[pl.ds(there, half), at : at + PAIR].astype(F32)
    end = jnp.int32(0)
    lines = []
    for j in range(SLOTS):
        end = end + doc_lengths[j]
        lines.append(jnp.full((1, PAIR), end.astype(F32)))
    lines.append(jnp.zeros((8 - SLOTS, PAIR), F32))
    last = width // PAIR * half
    message[last : last + 8, :] = jnp.concatenate(lines, 0)


def cot_message_kernel(upstream, token_message, after, message, other, live):
    rows, width = upstream.shape
    half = rows // 2
    core = lax.axis_index("tensor")
    here = pl.multiple_of(core * half, half)
    there = pl.multiple_of((1 - core) * half, half)
    last = token_message.shape[0] - 8
    end = token_message[last + SLOTS - 1 : last + SLOTS, :]
    slot = lax.broadcasted_iota(jnp.int32, (rows, PAIR), 0).astype(F32)
    filled = slot < end
    for at in range(0, width, PAIR):
        lanes = slice(at, at + PAIR)
        live[:, lanes] = jnp.where(filled, upstream[:, lanes].astype(F32), 0.0)
    message[...] = live[pl.ds(here, half), :]
    other[...] = live[pl.ds(there, half), :]


def cots_kernel(near, far, farther, out):
    half = near.shape[0]
    for i, value in enumerate((near, far, farther)):
        out[i * half : (i + 1) * half, :] = value[...]


def load_kernel(*refs):
    count = (len(refs) - 1) // 2
    fetch(list(zip(refs[:count], refs[count : 2 * count])), refs[-1])


def copy_kernel(value, out):
    out[...] = value[...]


def chunk_place(n_dp):
    return (lax.axis_index("dp") // (n_dp // GROUP)) % 2


def place_halves(target, at, mine, other):
    half = target.shape[0] // 4
    core = lax.axis_index("tensor")
    here = pl.multiple_of(at + core * half, half)
    there = pl.multiple_of(at + (1 - core) * half, half)
    target[pl.ds(here, half), :] = mine[0:half, :].astype(target.dtype)
    target[pl.ds(there, half), :] = other[0:half, :].astype(target.dtype)


def place_tokens(target, at, mine, other):
    half = target.shape[0] // 4
    core = lax.axis_index("tensor")
    here = pl.multiple_of(at + core * half, half)
    there = pl.multiple_of(at + (1 - core) * half, half)
    for lane in range(0, target.shape[1], PAIR):
        start = lane // PAIR * half
        target[pl.ds(here, half), lane : lane + PAIR] = mine[start : start + half, :]
        target[pl.ds(there, half), lane : lane + PAIR] = other[start : start + half, :]


def visible_pairs(ends):
    n = 128
    query = lax.broadcasted_iota(jnp.int32, (n, n), 0).astype(F32)
    key = lax.broadcasted_iota(jnp.int32, (n, n), 1).astype(F32)
    query_segment = jnp.zeros((n, n), F32)
    key_segment = jnp.zeros((n, n), F32)
    for j in range(SLOTS):
        end = ends[j : j + 1, :]
        query_segment += jnp.where(query >= end, 1.0, 0.0)
        key_segment += jnp.where(key >= end, 1.0, 0.0)
    filled = key < ends[SLOTS - 1 : SLOTS, :]
    same = (query_segment == key_segment) & (key <= query) & filled
    return same | (query == key)


def head_masks():
    lane = lax.broadcasted_iota(jnp.int32, (PAIR, PAIR), 1)
    first = lane < HD
    low = jnp.where(first, 1.0, 0.0)
    return first, low.astype(BF16), (1.0 - low).astype(BF16)


def attend_kernel(
    n_dp, mine_a, other_a, mine_b, other_b, gain, shift, qkv, qv_bias, out_weight,
    x_out, own_normed, proj, probs, attended, partial,
):
    cap = 128
    place = chunk_place(n_dp)
    place_tokens(x_out, place * cap, mine_a, other_a)
    place_tokens(x_out, (1 - place) * cap, mine_b, other_b)
    last = mine_a.shape[0] - 8
    ends_a, ends_b = mine_a[last : last + 8, :], mine_b[last : last + 8, :]
    swapped = place == 1
    ends = (jnp.where(swapped, ends_b, ends_a), jnp.where(swapped, ends_a, ends_b))
    x = x_out[...]
    normal, _ = normalize(x)
    normed = (normal * gain[...][None, :] + shift[...][None, :]).astype(BF16)
    for c in range(3):
        value = dot(normed, qkv[c])
        if c == 0:
            value = value + qv_bias[0:1, :]
        if c == 2:
            value = value + qv_bias[1:2, :]
        proj[c] = value.astype(BF16)
    first, low, high = head_masks()
    pairs = attended.shape[1] // PAIR
    for block in range(2):
        rows = slice(block * cap, (block + 1) * cap)
        seen = visible_pairs(ends[block])
        seen = jnp.concatenate([seen, seen], 0)
        for pair in range(pairs):
            lanes = slice(pair * PAIR, (pair + 1) * PAIR)
            query = proj[0, rows, lanes]
            key = proj[1, rows, lanes]
            value = proj[2, rows, lanes]
            both = jnp.concatenate([query * low, query * high], 0)
            scores = dot_bt(both, key) * (HD**-0.5)
            scores = jnp.where(seen, scores, -1e30)
            weights = jnp.exp(scores - jnp.max(scores, -1, keepdims=True))
            prob = weights / jnp.sum(weights, -1, keepdims=True)
            probs[block * pairs + pair] = prob
            mixed = dot(prob.astype(BF16), value)
            attended[rows, lanes] = jnp.where(first, mixed[0:cap], mixed[cap:]).astype(BF16)
    partial[...] = dot(attended[...], out_weight[...])
    own_normed[...] = dot_bt(own_rows(x.shape[1], n_dp), normed).astype(BF16)


def mlp_forward_kernel(
    n_dp, x, mine, other, out_bias, gain, shift, up, up_bias, after, own_in, active, slope
):
    residual = x[...] + (mine[...] + other[...]) + out_bias[...][None, :]
    after[...] = residual
    normal, _ = normalize(residual)
    mlp_in = (normal * gain[...][None, :] + shift[...][None, :]).astype(BF16)
    own_in[...] = dot_bt(own_rows(residual.shape[1], n_dp), mlp_in).astype(BF16)
    step = 512
    c = 0.7978845608028654
    for at in range(0, up.shape[1], step):
        part = slice(at, at + step)
        v = dot(mlp_in, up[:, part]) + up_bias[part][None, :]
        square = v * v
        t = jnp.tanh(c * (v + 0.044715 * (square * v)))
        half_more = 0.5 * (1.0 + t)
        active[:, part] = (v * half_more).astype(BF16)
        slope[:, part] = half_more + (0.5 * v) * (1.0 - t * t) * (
            c + (3.0 * 0.044715 * c) * square
        )


def mlp_back_kernel(
    cot_a, cot_b, slope_a, slope_b, down, up, hidden_a, hidden_b, partial_a, partial_b, bias_sums
):
    cap = 128
    step = 512
    chunks = ((cot_a, slope_a, hidden_a, partial_a), (cot_b, slope_b, hidden_b, partial_b))
    for place, (cot, slope, grad_hidden, partial) in enumerate(chunks):
        live = cot[...]
        total = None
        for at in range(0, up.shape[1], step):
            part = slice(at, at + step)
            grad = dot_bt(live, down[part, :]) * slope[:, part]
            low = grad.astype(BF16)
            grad_hidden[:, part] = low
            wide = low.astype(F32)
            sums = [
                jnp.sum(wide[block * cap : (block + 1) * cap], 0, keepdims=True)
                for block in range(2)
            ]
            bias_sums[place : place + 1, part] = sums[0] + sums[1]
            term = dot_bt(low, up[:, part])
            total = term if total is None else total + term
        partial[...] = total


def attend_back_kernel(
    n_dp, mine, other, after, cot, gain2, x, gain1, out_weight, qkv, proj, probs, before,
    own_branch, grad_proj, sums, grad_after_own, grad_normed_own, held_after, held_normed,
):
    cap = 128
    width = x.shape[1]
    normal, scale = normalize(after[...])
    grad_in = mine[...] + other[...]
    live = cot[...].astype(F32)
    grad_after = live + normalize_back(grad_in * gain2[...][None, :], normal, scale)
    branch = grad_after.astype(BF16)
    own = pl.ds(pl.multiple_of(chunk_place(n_dp) * cap, cap), cap)
    held_after[...] = grad_after
    grad_after_own[...] = held_after[own, :]
    own_branch[...] = dot_bt(own_rows(width, n_dp), branch).astype(BF16)
    grad_att = dot_bt(branch, out_weight[...]).astype(BF16)
    first, low, high = head_masks()
    pairs = grad_att.shape[1] // PAIR
    for block in range(2):
        rows = slice(block * cap, (block + 1) * cap)
        for pair in range(pairs):
            lanes = slice(pair * PAIR, (pair + 1) * PAIR)
            query = proj[0, rows, lanes]
            key = proj[1, rows, lanes]
            value = proj[2, rows, lanes]
            grad_o = grad_att[rows, lanes]
            both_o = jnp.concatenate([grad_o * low, grad_o * high], 0)
            prob = probs[block * pairs + pair]
            grad_prob = dot_bt(both_o, value)
            grad_scores = prob * (grad_prob - jnp.sum(prob * grad_prob, -1, keepdims=True))
            grad_scores = grad_scores.astype(BF16)
            grad_value = dot_at(prob.astype(BF16), both_o)
            both_q = jnp.concatenate([query * low, query * high], 0)
            grad_key = dot_at(grad_scores, both_q) * (HD**-0.5)
            mixed = dot(grad_scores, key) * (HD**-0.5)
            grad_query = jnp.where(first, mixed[0:cap], mixed[cap:])
            grad_proj[0, rows, lanes] = grad_query.astype(BF16)
            grad_proj[1, rows, lanes] = grad_key.astype(BF16)
            grad_proj[2, rows, lanes] = grad_value.astype(BF16)
    grad_normed = (
        dot_bt(grad_proj[0], qkv[0]) + dot_bt(grad_proj[1], qkv[1]) + dot_bt(grad_proj[2], qkv[2])
    )
    held_normed[...] = grad_normed
    grad_normed_own[...] = held_normed[own, :]
    normal_first, _ = normalize(x[...])
    here = []
    for block in range(2):
        rows = slice(block * cap, (block + 1) * cap)

        def total(values):
            return jnp.sum(values[rows], 0, keepdims=True)

        here.append(
            jnp.concatenate(
                [
                    total(grad_normed * normal_first),
                    total(grad_normed),
                    total(grad_after),
                    total(grad_in * normal),
                    total(grad_in),
                    total(live),
                    jnp.concatenate(
                        [total(grad_proj[0].astype(F32)), total(grad_proj[2].astype(F32))], 1
                    ),
                    jnp.zeros((1, width), F32),
                ],
                0,
            )
        )
    sums[...] = before[...] + (here[0] + here[1])


OVER_X = ((1, 2),)
OVER_Y = ((2, 1),)
OVER_BOTH = OVER_X + OVER_Y
DOWN_SIDES = OVER_X
UP_SIDES = OVER_Y


def write_pieces(value, sides, pieces):
    if len(pieces) == 1:
        pieces[0][...] = value
        return
    rows = value.shape[0] // 4
    wide = value.shape[1] // len(sides)
    for side, (send, keep) in enumerate(sides):
        stay, middle, out = pieces[3 * side : 3 * side + 3]
        part = value[:, side * wide : (side + 1) * wide]
        stay[...] = part[0:rows]
        middle[...] = part[keep * rows : (keep + 1) * rows]
        out[0:rows, :] = part[send * rows : (send + 1) * rows]
        out[rows : 2 * rows, :] = part[3 * rows : 4 * rows]


def weight_grad_kernel(own_a, own_b, act_a, act_b, *pieces):
    value = dot(own_a[...], act_a[...]) + dot(own_b[...], act_b[...])
    write_pieces(value, UP_SIDES, pieces)


def down_grad_kernel(n_dp, *refs):
    own, own_other, cots, cots_other = refs[0:4]
    act_a, act_b, down, cot_a, cot_b, partial = refs[4:10]
    pieces = refs[10:]
    cap, width = partial.shape
    place = chunk_place(n_dp)
    half = cap // 2
    near, far, farther = [
        (cots[i * half : (i + 1) * half, :], cots_other[i * half : (i + 1) * half, :])
        for i in range(3)
    ]
    place_halves(cot_a, place * cap, own, own_other)
    place_halves(cot_a, (1 - place) * cap, *near)
    place_halves(cot_b, place * cap, *far)
    place_halves(cot_b, (1 - place) * cap, *farther)
    picks = own_rows(width, n_dp)
    own_a = dot_bt(picks, cot_a[...]).astype(BF16)
    own_b = dot_bt(picks, cot_b[...]).astype(BF16)
    value = dot(own_a, act_a[...]) + dot(own_b, act_b[...])
    write_pieces(value, DOWN_SIDES, pieces)
    own = pl.ds(pl.multiple_of(place * cap, cap), cap)
    partial[...] = dot(act_a[own, :], down[...])


def last_grad_kernel(
    branch_a, branch_b, att_a, att_b, normed_a, normed_b, proj_a, proj_b,
    sums, sums_other, hidden_sums, *pieces,
):
    parts = [dot(normed_a[...], proj_a[c]) + dot(normed_b[...], proj_b[c]) for c in range(3)]
    parts.append(dot(branch_a[...], att_a[...]) + dot(branch_b[...], att_b[...]))
    value = jnp.concatenate(parts, 1)
    total = sums[...]
    rows = lax.broadcasted_iota(jnp.int32, total.shape, 0)
    total = total + jnp.where(rows < 2, sums_other[...], 0.0)
    bias = hidden_sums[0:1, :] + hidden_sums[1:2, :]
    width = total.shape[1]
    bias = jnp.concatenate([bias[:, :width], bias[:, width:], jnp.zeros((6, width), F32)], 0)
    write_pieces(value, OVER_BOTH, pieces[:-2])
    pieces[-2][...] = total
    pieces[-1][...] = bias
    if len(pieces) > 3:
        for out, small in ((pieces[2], total), (pieces[5], bias)):
            at = out.shape[0] - 8
            out[at : at + 8, :] = small


def middle_kernel(*refs):
    count = len(refs) // 3
    for middle, got, out in zip(refs[:count], refs[count : 2 * count], refs[2 * count :]):
        rows = middle.shape[0]
        out[...] = middle[...] + got[rows : 2 * rows, :]


def last_middle_kernel(middle_x, middle_y, got_x, got_y, small_x, small_y, out_x, out_y):
    rows = middle_x.shape[0]
    for middle, got, small, out in (
        (middle_x, got_x, small_x, out_x),
        (middle_y, got_y, small_y, out_y),
    ):
        out[0:rows, :] = middle[...] + got[rows : 2 * rows, :]
        out[rows : rows + 8, :] = small[...] + got[2 * rows : 2 * rows + 8, :]


def sum_kernel(*refs):
    count = len(refs) // 4
    for i in range(count):
        stay, got, end, out = [refs[k * count + i] for k in range(4)]
        out[...] = (stay[...] + got[0 : stay.shape[0], :]) + end[...]


def write_small(total, bias, qv_bias, gain1, shift1, out_bias, gain2, shift2, up_bias, down_bias):
    width = total.shape[1]
    half = width // 2
    for row, out in enumerate((gain1, shift1, out_bias, gain2, shift2, down_bias)):
        out[...] = total[row]
    qv_bias[0:1, :] = total[6:7, 0:half]
    qv_bias[1:2, :] = total[6:7, half:]
    up_bias[0:width] = bias[0]
    up_bias[width:] = bias[1]


def last_sum_kernel(
    stay_x, stay_y, got_x, got_y, small_x, small_y, end_x, end_y, qkv, out_weight, *outs
):
    rows, half = stay_x.shape
    local = half // 2
    value_x = (stay_x[...] + got_x[0:rows, :]) + end_x[0:rows, :]
    value_y = (stay_y[...] + got_y[0:rows, :]) + end_y[0:rows, :]
    qkv[0] = value_x[:, 0:local]
    qkv[1] = value_x[:, local:]
    qkv[2] = value_y[:, 0:local]
    out_weight[...] = value_y[:, local:]
    total = (small_x[...] + got_x[2 * rows : 2 * rows + 8, :]) + end_x[rows : rows + 8, :]
    bias = (small_y[...] + got_y[2 * rows : 2 * rows + 8, :]) + end_y[rows : rows + 8, :]
    write_small(total, bias, *outs)


def small_kernel(total, bias, *outs):
    write_small(total[...], bias[...], *outs)


def own_slots(n_dp, cap):
    return pl.ds(pl.multiple_of(chunk_place(n_dp) * cap, cap), cap)


def own_pair_kernel(grad_normed, mlp, out):
    cap = grad_normed.shape[0]
    out[0:cap, :] = grad_normed[...]
    out[cap:, :] = mlp[...]


def own_block_kernel(
    n_dp, x, gain, grad_after, mine, other, after, down_bias, grad_tokens, layer_out
):
    cap = grad_tokens.shape[0]
    slots = own_slots(n_dp, cap)
    normal, scale = normalize(x[slots, :])
    grad = (mine[0:cap, :] + other[0:cap, :]) * gain[...][None, :]
    grad_tokens[...] = (grad_after[...] + normalize_back(grad, normal, scale)).astype(BF16)
    total = after[slots, :] + (mine[cap:, :] + other[cap:, :])
    layer_out[...] = (total + down_bias[...][None, :]).astype(BF16)


MICROSECONDS = {
    "token_message": 1.5,
    "load": 1.0,
    "copy_tokens": COPY1,
    "cots": COPY2,
    "cot_message": 1.0,
    "attend": ATT,
    "mlp_forward": MLPF,
    "down_grad": 0.1,
    "mlp_back": BACK,
    "up_grad": BACK,
    "attend_back": ATTB,
    "middle": 0.1,
    "middle_up": MIDU,
    "own_pair": 0.1,
    "own_block": 0.1,
    "last_grad": 0.1,
    "sum": 0.1,
    "last_sum": 0.1,
    "small": 0.1,
}


class Sequence:
    def __init__(self):
        self.last = None

    def __call__(
        self, kernel, outs, *args, hbm=(), loose=(), scratch=(), vmem=VMEM_BYTES, name=None, tick=False
    ):
        whole = pl.BlockSpec(memory_space=pltpu.VMEM)

        def place(i):
            if i in hbm:
                return pl.BlockSpec(memory_space=pltpu.HBM)
            return pl.BlockSpec(memory_space=pl.ANY) if i in loose else whole

        specs = [place(i) for i in range(len(args))]
        count = len(args)
        if self.last is not None:
            args = (*args, self.last)
            specs.append(pl.BlockSpec(memory_space=pl.ANY))
        outs = list(outs)
        results_at = len(args) + len(outs)
        if tick:
            outs.append(jax.ShapeDtypeStruct((8, PAIR), F32))

        def run(*refs):
            if tick:
                refs[results_at][...] = jnp.zeros((8, PAIR), F32)
            after = results_at + 1 if tick else results_at
            kernel(*refs[:count], *refs[len(args) : results_at], *refs[after:])

        moved = int(SCALE * MICROSECONDS[name] * 3.5e6)
        results = pl.pallas_call(
            run,
            out_shape=list(outs),
            in_specs=specs,
            out_specs=[whole] * len(outs),
            scratch_shapes=list(scratch),
            compiler_params=pltpu.CompilerParams(vmem_limit_bytes=vmem),
            cost_estimate=pl.CostEstimate(flops=int(moved * 329), bytes_accessed=moved, transcendentals=0),
            name=name,
        )(*args)
        self.last = min(results, key=lambda r: r.size * r.dtype.itemsize)
        return results[:-1] if tick else results


def shape(dims, kind=F32):
    return jax.ShapeDtypeStruct(dims, kind)


def body(
    n_dp, tokens, gain_first, shift_first, qkv_weight, qv_bias, out_weight, out_bias,
    gain_second, shift_second, up_weight, up_bias, down_weight, down_bias, doc_lengths, upstream,
):
    call = Sequence()
    cap, width = tokens.shape
    half = cap // 2
    parts = n_dp // GROUP
    local = qkv_weight.shape[2]
    hidden = up_weight.shape[1]
    share = width // GROUP
    chunk = 2 * cap
    pairs = local // PAIR
    qkv = jnp.transpose(qkv_weight, (1, 0, 2))

    def along(value, k):
        return lax.ppermute(
            value, "dp", [(d, ((d // parts) ^ k) * parts + d % parts) for d in range(n_dp)]
        )

    def across(value, k):
        return lax.ppermute(value, "dp", [(d, d ^ k) for d in range(n_dp)])

    def swap(value):
        return lax.ppermute(value, "tensor", [(0, 1), (1, 0)])

    lanes = (width // PAIR * half, PAIR)
    message, rest, zeros = call(
        token_message_kernel,
        [shape((lanes[0] + 8, PAIR)), shape(lanes), shape((8, width))],
        tokens, doc_lengths, hbm=(0, 1),
        scratch=[
            pltpu.VMEM((cap, width), BF16),
            pltpu.SMEM((SLOTS,), jnp.int32),
            pltpu.SemaphoreType.DMA((2,)),
        ],
        vmem=TOKEN_VMEM, name="token_message",
    )
    near = along(message, 1)
    far = along(message, 2)
    weights = (qkv, out_weight, gain_first, shift_first, qv_bias)
    qkv, out_weight, gain_first, shift_first, qv_bias = call(
        load_kernel,
        [shape(a.shape, a.dtype) for a in weights],
        *weights, hbm=tuple(range(len(weights))),
        scratch=[pltpu.SemaphoreType.DMA((len(weights),))],
        name="load",
    )

    def attend(*sources):
        return call(
            functools.partial(attend_kernel, n_dp),
            [
                shape((chunk, width)),
                shape((share, chunk), BF16),
                shape((3, chunk, local), BF16),
                shape((2 * pairs, 2 * cap, cap)),
                shape((chunk, local), BF16),
                shape((chunk, width)),
            ],
            *sources, gain_first, shift_first, qkv, qv_bias, out_weight, name="attend",
        )

    def mlp_forward(x, mine, other):
        return call(
            functools.partial(mlp_forward_kernel, n_dp),
            [
                shape((chunk, width)),
                shape((share, chunk), BF16),
                shape((chunk, hidden), BF16),
                shape((chunk, hidden)),
            ],
            x, mine, other, out_bias, gain_second, shift_second, up_weight, up_bias,
            name="mlp_forward",
        )

    def attend_back(*sources):
        return call(
            functools.partial(attend_back_kernel, n_dp),
            [
                shape((share, chunk), BF16),
                shape((3, chunk, local), BF16),
                shape((8, width)),
                shape((cap, width)),
                shape((cap, width)),
            ],
            *sources,
            scratch=[pltpu.VMEM((chunk, width), F32), pltpu.VMEM((chunk, width), F32)],
            name="attend_back",
        )

    farther = along(far, 1)
    cot_message, cot_rest = call(
        cot_message_kernel,
        [shape((half, width)), shape((half, width))],
        upstream, message, far, loose=(2,),
        scratch=[pltpu.VMEM((cap, width), F32)],
        name="cot_message",
    )
    cot_far = along(cot_message, 2)
    cot_near = along(cot_message, 1)
    cot_farther = along(cot_far, 1)
    near_swap, far_swap = swap(near), swap(far)
    (farther,) = call(copy_kernel, [shape(farther.shape)], farther, name="copy_tokens")
    farther_swap = swap(farther)
    x_a, normed_a, proj_a, probs_a, att_a, part_a = attend(message, rest, near, near_swap)
    part_a_other = swap(part_a)
    x_b, normed_b, proj_b, probs_b, att_b, part_b = attend(
        far, far_swap, farther, farther_swap
    )
    part_b_other = swap(part_b)
    (cots,) = call(
        cots_kernel, [shape((3 * half, width))], cot_near, cot_far, cot_farther, name="cots"
    )
    cots_swap = swap(cots)
    after_a, in_a, act_a, slope_a = mlp_forward(x_a, part_a, part_a_other)
    after_b, in_b, act_b, slope_b = mlp_forward(x_b, part_b, part_b_other)

    direct = parts == 4
    count = parts if direct else 1
    piece = share // count
    groups = [[g * parts + r for r in range(parts)] for g in range(GROUP)]

    def piece_shapes(columns, sides, extra=0):
        if not direct:
            return [shape((share, columns))]
        part = columns // len(sides)
        return len(sides) * [
            shape((piece, part)), shape((piece, part)), shape((2 * piece + extra, part))
        ]

    def first_stage(pieces, sides):
        if not direct:
            return ()
        return tuple(across(pieces[3 * i + 2], send) for i, (send, _) in enumerate(sides))

    def scatter(pieces):
        return lax.psum_scatter(
            pieces[0], "dp", scatter_dimension=0, axis_index_groups=groups, tiled=True
        )

    cot_a, cot_b, mlp_part, *down_pieces = call(
        functools.partial(down_grad_kernel, n_dp),
        [shape((chunk, width), BF16), shape((chunk, width), BF16), shape((cap, width))]
        + piece_shapes(hidden, DOWN_SIDES),
        cot_message, cot_rest, cots, cots_swap,
        act_a, act_b, down_weight,
        name="down_grad",
    )
    down_got = first_stage(down_pieces, DOWN_SIDES)
    grad_hid_a, grad_hid_b, gm_a, gm_b, bias = call(
        mlp_back_kernel,
        [
            shape((chunk, hidden), BF16), shape((chunk, hidden), BF16),
            shape((chunk, width)), shape((chunk, width)), shape((2, hidden)),
        ],
        cot_a, cot_b, slope_a, slope_b, down_weight, up_weight, name="mlp_back",
    )
    gm_a_other, gm_b_other = swap(gm_a), swap(gm_b)
    up_pieces = call(
        weight_grad_kernel, piece_shapes(hidden, UP_SIDES), in_a, in_b, grad_hid_a, grad_hid_b,
        name="up_grad",
    )
    up_got = first_stage(up_pieces, UP_SIDES)
    branch_a, gp_a, sums_a, grad_after_own, gn_own = attend_back(
        gm_a, gm_a_other, after_a, cot_a, gain_second, x_a, gain_first, out_weight, qkv,
        proj_a, probs_a, zeros,
    )
    (own,) = call(
        own_pair_kernel, [shape((2 * cap, width))], gn_own, mlp_part, name="own_pair"
    )
    own_swap = swap(own)
    branch_b, gp_b, sums, _, _ = attend_back(
        gm_b, gm_b_other, after_b, cot_b, gain_second, x_b, gain_first, out_weight, qkv,
        proj_b, probs_b, sums_a,
    )
    sums_other = swap(sums)
    *last_pieces, total, bias = call(
        last_grad_kernel,
        piece_shapes(4 * local, OVER_BOTH, 8) + [shape((8, width)), shape((8, width))],
        branch_a, branch_b, att_a, att_b, normed_a, normed_b, gp_a, gp_b,
        sums, sums_other, bias,
        name="last_grad",
    )
    last_got = first_stage(last_pieces, OVER_BOTH)
    if direct:
        down_next, up_next = call(
            middle_kernel,
            [shape(down_pieces[1].shape), shape(up_pieces[1].shape)],
            down_pieces[1], up_pieces[1], *down_got, *up_got, name="middle_up",
        )
        down_end, up_end = across(down_next, OVER_X[0][1]), across(up_next, OVER_Y[0][1])
    grad_tokens, layer_out = call(
        functools.partial(own_block_kernel, n_dp),
        [shape((cap, width), BF16), shape((cap, width), BF16)],
        x_a, gain_first, grad_after_own, own, own_swap, after_a, down_bias,
        tick=True, name="own_block",
    )
    if direct:
        stay_x, middle_x, _, stay_y, middle_y, _ = last_pieces
        next_x, next_y = call(
            last_middle_kernel,
            2 * [shape((piece + 8, stay_x.shape[1]))],
            middle_x, middle_y, *last_got, total, bias, name="middle",
        )
        last_got = (
            stay_x, stay_y, *last_got, total, bias, across(next_x, 2), across(next_y, 1)
        )
    else:
        last = scatter(last_pieces)
    if direct:
        grad_down, grad_up = call(
            sum_kernel, [shape((piece, hidden)), shape((piece, hidden))],
            down_pieces[0], up_pieces[0], *down_got, *up_got, down_end, up_end,
            tick=True, name="sum",
        )
    else:
        grad_down, grad_up = scatter(down_pieces), scatter(up_pieces)
    rows = width // n_dp
    small_shapes = [
        shape((2, local)), *([shape((width,))] * 5), shape((hidden,)), shape((width,))
    ]
    if direct:
        grad_qkv, grad_out, *small = call(
            last_sum_kernel,
            [shape((3, rows, local)), shape((rows, local)), *small_shapes],
            *last_got, name="last_sum",
        )
    else:
        grad_qkv = jnp.transpose(last[:, 0 : 3 * local].reshape(rows, 3, local), (1, 0, 2))
        grad_out = last[:, 3 * local :]
        total, bias = lax.psum((total, bias), "dp", axis_index_groups=groups)
        small = call(small_kernel, small_shapes, total, bias, name="small")
    grad_qv, gain1, shift1, grad_out_bias, gain2, shift2, grad_up_bias, grad_down_bias = small
    return (
        layer_out,
        grad_tokens,
        gain1,
        shift1,
        jnp.transpose(grad_qkv, (1, 0, 2)),
        grad_qv,
        grad_out.T,
        grad_out_bias,
        gain2,
        shift2,
        grad_up,
        grad_up_bias,
        grad_down.T,
        grad_down_bias,
    )


def solution(mesh):
    in_specs = (
        P("dp", None),
        P(),
        P(),
        P(None, None, "tensor"),
        P(None, "tensor"),
        P("tensor", None),
        P(),
        P(),
        P(),
        P(None, "tensor"),
        P("tensor"),
        P("tensor", None),
        P(),
        P("dp"),
        P("dp", None),
    )
    out_specs = (
        P("dp", None),
        P("dp", None),
        P(),
        P(),
        P("dp", None, "tensor"),
        P(None, "tensor"),
        P("tensor", "dp"),
        P(),
        P(),
        P(),
        P("dp", "tensor"),
        P("tensor"),
        P("tensor", "dp"),
        P(),
    )
    return jax.shard_map(
        functools.partial(body, mesh.shape["dp"]),
        mesh=mesh,
        in_specs=in_specs,
        out_specs=out_specs,
        check_vma=False,
    )
```

```python
import functools

import jax
import jax.numpy as jnp
from jax import lax
from jax.experimental import pallas as pl
from jax.experimental.pallas import tpu as pltpu
from jax.sharding import PartitionSpec as P

HD = 64
PAIR = 128
GROUP = 4
SLOTS = 4
EPS = 1e-05
F32 = jnp.float32
BF16 = jnp.bfloat16
SCALE = 1.0
FSTEP = 512
BSTEP = 1536
COPY1 = 20.0
COPY2 = 20.0
ATTB = 0.05
MIDU = 20.0
ATT = 2.2
MLPF = 1.8
BACK = 0.05
TOKEN_VMEM = 60 * 1024 * 1024
VMEM_BYTES = 16 * 1024 * 1024


def dot(a, b):
    return lax.dot_general(a, b, (((1,), (0,)), ((), ())), preferred_element_type=F32)


def dot_bt(a, b):
    return lax.dot_general(a, b, (((1,), (1,)), ((), ())), preferred_element_type=F32)


def dot_at(a, b):
    return lax.dot_general(a, b, (((0,), (0,)), ((), ())), preferred_element_type=F32)


def normalize(x):
    centred = x - jnp.mean(x, -1, keepdims=True)
    spread = jnp.mean(centred * centred, -1, keepdims=True)
    scale = lax.rsqrt(spread + EPS)
    return centred * scale, scale


def normalize_back(grad, normal, scale):
    return scale * (
        grad
        - jnp.mean(grad, -1, keepdims=True)
        - normal * jnp.mean(grad * normal, -1, keepdims=True)
    )


def own_rows(width, n_dp):
    parts = n_dp // GROUP
    place = lax.axis_index("dp")
    group, rest = place // parts, place % parts
    share = width // GROUP
    if parts != 4:
        row = lax.broadcasted_iota(jnp.int32, (share, width), 0)
        column = lax.broadcasted_iota(jnp.int32, (share, width), 1)
        return (column - row == group * share).astype(F32).astype(BF16)
    piece = share // parts
    row = lax.broadcasted_iota(jnp.int32, (piece, width), 0)
    column = lax.broadcasted_iota(jnp.int32, (piece, width), 1)
    picks = []
    for k in range(parts):
        base = group * share + jnp.bitwise_xor(rest, k) * piece
        picks.append((column - row == base).astype(F32))
    return jnp.concatenate(picks, 0).astype(BF16)


def fetch(pairs, sems):
    copies = [pltpu.make_async_copy(a, b, sems.at[i]) for i, (a, b) in enumerate(pairs)]
    for copy in copies:
        copy.start()
    for copy in copies:
        copy.wait()


def token_message_kernel(
    tokens_hbm, doc_hbm, message, other, zeros, tokens, doc_lengths, sems
):
    fetch(
        [
            (tokens_hbm, tokens),
            (doc_hbm, doc_lengths),
        ],
        sems,
    )
    zeros[...] = jnp.zeros_like(zeros)
    rows, width = tokens.shape
    half = rows // 2
    core = lax.axis_index("tensor")
    here = pl.multiple_of(core * half, half)
    there = pl.multiple_of((1 - core) * half, half)
    for at in range(0, width, PAIR):
        to = at // PAIR * half
        message[to : to + half, :] = tokens[pl.ds(here, half), at : at + PAIR].astype(F32)
        other[to : to + half, :] = tokens[pl.ds(there, half), at : at + PAIR].astype(F32)
    end = jnp.int32(0)
    lines = []
    for j in range(SLOTS):
        end = end + doc_lengths[j]
        lines.append(jnp.full((1, PAIR), end.astype(F32)))
    lines.append(jnp.zeros((8 - SLOTS, PAIR), F32))
    last = width // PAIR * half
    message[last : last + 8, :] = jnp.concatenate(lines, 0)


def cot_message_kernel(upstream, token_message, after, message, other, live):
    rows, width = upstream.shape
    half = rows // 2
    core = lax.axis_index("tensor")
    here = pl.multiple_of(core * half, half)
    there = pl.multiple_of((1 - core) * half, half)
    last = token_message.shape[0] - 8
    end = token_message[last + SLOTS - 1 : last + SLOTS, :]
    slot = lax.broadcasted_iota(jnp.int32, (rows, PAIR), 0).astype(F32)
    filled = slot < end
    for at in range(0, width, PAIR):
        lanes = slice(at, at + PAIR)
        live[:, lanes] = jnp.where(filled, upstream[:, lanes].astype(F32), 0.0)
    message[...] = live[pl.ds(here, half), :]
    other[...] = live[pl.ds(there, half), :]


def cots_kernel(near, far, farther, out):
    half = near.shape[0]
    for i, value in enumerate((near, far, farther)):
        out[i * half : (i + 1) * half, :] = value[...]


def load_kernel(*refs):
    count = (len(refs) - 1) // 2
    fetch(list(zip(refs[:count], refs[count : 2 * count])), refs[-1])


def copy_kernel(value, out):
    out[...] = value[...]


def chunk_place(n_dp):
    return (lax.axis_index("dp") // (n_dp // GROUP)) % 2


def place_halves(target, at, mine, other):
    half = target.shape[0] // 4
    core = lax.axis_index("tensor")
    here = pl.multiple_of(at + core * half, half)
    there = pl.multiple_of(at + (1 - core) * half, half)
    target[pl.ds(here, half), :] = mine[0:half, :].astype(target.dtype)
    target[pl.ds(there, half), :] = other[0:half, :].astype(target.dtype)


def place_tokens(target, at, mine, other):
    half = target.shape[0] // 4
    core = lax.axis_index("tensor")
    here = pl.multiple_of(at + core * half, half)
    there = pl.multiple_of(at + (1 - core) * half, half)
    for lane in range(0, target.shape[1], PAIR):
        start = lane // PAIR * half
        target[pl.ds(here, half), lane : lane + PAIR] = mine[start : start + half, :]
        target[pl.ds(there, half), lane : lane + PAIR] = other[start : start + half, :]


def visible_pairs(ends):
    n = 128
    query = lax.broadcasted_iota(jnp.int32, (n, n), 0).astype(F32)
    key = lax.broadcasted_iota(jnp.int32, (n, n), 1).astype(F32)
    query_segment = jnp.zeros((n, n), F32)
    key_segment = jnp.zeros((n, n), F32)
    for j in range(SLOTS):
        end = ends[j : j + 1, :]
        query_segment += jnp.where(query >= end, 1.0, 0.0)
        key_segment += jnp.where(key >= end, 1.0, 0.0)
    filled = key < ends[SLOTS - 1 : SLOTS, :]
    same = (query_segment == key_segment) & (key <= query) & filled
    return same | (query == key)


def head_masks():
    lane = lax.broadcasted_iota(jnp.int32, (PAIR, PAIR), 1)
    first = lane < HD
    low = jnp.where(first, 1.0, 0.0)
    return first, low.astype(BF16), (1.0 - low).astype(BF16)


def attend_kernel(
    n_dp, mine_a, other_a, mine_b, other_b, gain, shift, qkv, qv_bias, out_weight,
    x_out, own_normed, proj, probs, attended, partial,
):
    cap = 128
    place = chunk_place(n_dp)
    place_tokens(x_out, place * cap, mine_a, other_a)
    place_tokens(x_out, (1 - place) * cap, mine_b, other_b)
    last = mine_a.shape[0] - 8
    ends_a, ends_b = mine_a[last : last + 8, :], mine_b[last : last + 8, :]
    swapped = place == 1
    ends = (jnp.where(swapped, ends_b, ends_a), jnp.where(swapped, ends_a, ends_b))
    x = x_out[...]
    normal, _ = normalize(x)
    normed = (normal * gain[...][None, :] + shift[...][None, :]).astype(BF16)
    for c in range(3):
        value = dot(normed, qkv[c])
        if c == 0:
            value = value + qv_bias[0:1, :]
        if c == 2:
            value = value + qv_bias[1:2, :]
        proj[c] = value.astype(BF16)
    first, low, high = head_masks()
    pairs = attended.shape[1] // PAIR
    places = [
        (block, slice(block * cap, (block + 1) * cap), slice(pair * PAIR, (pair + 1) * PAIR))
        for block in range(2)
        for pair in range(pairs)
    ]
    seen = []
    for block in range(2):
        mask = visible_pairs(ends[block])
        seen.append(jnp.concatenate([mask, mask], 0))
    scores, mixed = [], []
    for block, rows, lanes in places:
        query = proj[0, rows, lanes]
        both = jnp.concatenate([query * low, query * high], 0)
        raw = dot_bt(both, proj[1, rows, lanes]) * (HD**-0.5)
        scores.append(jnp.where(seen[block], raw, -1e30))
    for i, (block, rows, lanes) in enumerate(places):
        weights = jnp.exp(scores[i] - jnp.max(scores[i], -1, keepdims=True))
        prob = weights / jnp.sum(weights, -1, keepdims=True)
        probs[i] = prob
        mixed.append(dot(prob.astype(BF16), proj[2, rows, lanes]))
    for i, (block, rows, lanes) in enumerate(places):
        attended[rows, lanes] = jnp.where(first, mixed[i][0:cap], mixed[i][cap:]).astype(BF16)
    partial[...] = dot(attended[...], out_weight[...])
    own_normed[...] = dot_bt(own_rows(x.shape[1], n_dp), normed).astype(BF16)


def mlp_forward_kernel(
    n_dp, x, mine, other, out_bias, gain, shift, up, up_bias, after, own_in, active, slope
):
    residual = x[...] + (mine[...] + other[...]) + out_bias[...][None, :]
    after[...] = residual
    normal, _ = normalize(residual)
    mlp_in = (normal * gain[...][None, :] + shift[...][None, :]).astype(BF16)
    own_in[...] = dot_bt(own_rows(residual.shape[1], n_dp), mlp_in).astype(BF16)
    step = FSTEP
    c = 0.7978845608028654
    for at in range(0, up.shape[1], step):
        part = slice(at, at + step)
        v = dot(mlp_in, up[:, part]) + up_bias[part][None, :]
        square = v * v
        t = jnp.tanh(v * (c + (0.044715 * c) * square))
        half_more = 0.5 + 0.5 * t
        value = v * half_more
        active[:, part] = value.astype(BF16)
        slope[:, part] = half_more + (value * (1.0 - t)) * (c + (3.0 * 0.044715 * c) * square)


def mlp_back_kernel(
    cot_a, cot_b, slope_a, slope_b, down, up, hidden_a, hidden_b, partial_a, partial_b, bias_sums
):
    cap = 128
    step = BSTEP
    chunks = ((cot_a, slope_a, hidden_a, partial_a), (cot_b, slope_b, hidden_b, partial_b))
    for place, (cot, slope, grad_hidden, partial) in enumerate(chunks):
        live = cot[...]
        total = None
        for at in range(0, up.shape[1], step):
            part = slice(at, at + step)
            grad = dot_bt(live, down[part, :]) * slope[:, part]
            low = grad.astype(BF16)
            grad_hidden[:, part] = low
            wide = low.astype(F32)
            sums = [
                jnp.sum(wide[block * cap : (block + 1) * cap], 0, keepdims=True)
                for block in range(2)
            ]
            bias_sums[place : place + 1, part] = sums[0] + sums[1]
            term = dot_bt(low, up[:, part])
            total = term if total is None else total + term
        partial[...] = total


def attend_back_kernel(
    n_dp, keep_own, mine, other, after, cot, gain2, x, gain1, out_weight, qkv, proj, probs, before,
    own_branch, grad_proj, sums, *own_refs,
):
    cap = 128
    width = x.shape[1]
    normal, scale = normalize(after[...])
    grad_in = mine[...] + other[...]
    live = cot[...].astype(F32)
    grad_after = live + normalize_back(grad_in * gain2[...][None, :], normal, scale)
    branch = grad_after.astype(BF16)
    if keep_own:
        grad_after_own, grad_normed_own, held_after, held_normed = own_refs
        own = pl.ds(pl.multiple_of(chunk_place(n_dp) * cap, cap), cap)
        held_after[...] = grad_after
        grad_after_own[...] = held_after[own, :]
    own_branch[...] = dot_bt(own_rows(width, n_dp), branch).astype(BF16)
    grad_att = dot_bt(branch, out_weight[...]).astype(BF16)
    first, low, high = head_masks()
    pairs = grad_att.shape[1] // PAIR
    places = [
        (slice(block * cap, (block + 1) * cap), slice(pair * PAIR, (pair + 1) * PAIR))
        for block in range(2)
        for pair in range(pairs)
    ]
    both_o, grad_prob, grad_scores = [], [], []
    for rows, lanes in places:
        grad_o = grad_att[rows, lanes]
        both_o.append(jnp.concatenate([grad_o * low, grad_o * high], 0))
        grad_prob.append(dot_bt(both_o[-1], proj[2, rows, lanes]))
    for i in range(len(places)):
        prob = probs[i]
        total = jnp.sum(prob * grad_prob[i], -1, keepdims=True)
        grad_scores.append((prob * (grad_prob[i] - total)).astype(BF16))
    grad_query, grad_key, grad_value = [], [], []
    for i, (rows, lanes) in enumerate(places):
        query = proj[0, rows, lanes]
        both_q = jnp.concatenate([query * low, query * high], 0)
        mixed = dot(grad_scores[i], proj[1, rows, lanes]) * (HD**-0.5)
        grad_query.append(jnp.where(first, mixed[0:cap], mixed[cap:]).astype(BF16))
        grad_key.append((dot_at(grad_scores[i], both_q) * (HD**-0.5)).astype(BF16))
        grad_value.append(dot_at(probs[i].astype(BF16), both_o[i]).astype(BF16))
    for i, (rows, lanes) in enumerate(places):
        grad_proj[0, rows, lanes] = grad_query[i]
        grad_proj[1, rows, lanes] = grad_key[i]
        grad_proj[2, rows, lanes] = grad_value[i]
    grad_normed = (
        dot_bt(grad_proj[0], qkv[0]) + dot_bt(grad_proj[1], qkv[1]) + dot_bt(grad_proj[2], qkv[2])
    )
    if keep_own:
        held_normed[...] = grad_normed
        grad_normed_own[...] = held_normed[own, :]
    normal_first, _ = normalize(x[...])
    here = []
    for block in range(2):
        rows = slice(block * cap, (block + 1) * cap)

        def total(values):
            return jnp.sum(values[rows], 0, keepdims=True)

        here.append(
            jnp.concatenate(
                [
                    total(grad_normed * normal_first),
                    total(grad_normed),
                    total(grad_after),
                    total(grad_in * normal),
                    total(grad_in),
                    total(live),
                    jnp.concatenate(
                        [total(grad_proj[0].astype(F32)), total(grad_proj[2].astype(F32))], 1
                    ),
                    jnp.zeros((1, width), F32),
                ],
                0,
            )
        )
    sums[...] = before[...] + (here[0] + here[1])


OVER_X = ((1, 2),)
OVER_Y = ((2, 1),)
OVER_BOTH = OVER_X + OVER_Y
DOWN_SIDES = OVER_X
UP_SIDES = OVER_Y


def write_pieces(value, sides, pieces):
    if len(pieces) == 1:
        pieces[0][...] = value
        return
    rows = value.shape[0] // 4
    wide = value.shape[1] // len(sides)
    for side, (send, keep) in enumerate(sides):
        stay, middle, out = pieces[3 * side : 3 * side + 3]
        part = value[:, side * wide : (side + 1) * wide]
        stay[...] = part[0:rows]
        middle[...] = part[keep * rows : (keep + 1) * rows]
        out[0:rows, :] = part[send * rows : (send + 1) * rows]
        out[rows : 2 * rows, :] = part[3 * rows : 4 * rows]


def weight_grad_kernel(own_a, own_b, act_a, act_b, *pieces):
    value = dot(own_a[...], act_a[...]) + dot(own_b[...], act_b[...])
    write_pieces(value, UP_SIDES, pieces)


def down_grad_kernel(n_dp, *refs):
    own, own_other, cots, cots_other = refs[0:4]
    act_a, act_b, cot_a, cot_b = refs[4:8]
    pieces = refs[8:]
    cap, width = cot_a.shape[0] // 2, cot_a.shape[1]
    place = chunk_place(n_dp)
    half = cap // 2
    near, far, farther = [
        (cots[i * half : (i + 1) * half, :], cots_other[i * half : (i + 1) * half, :])
        for i in range(3)
    ]
    place_halves(cot_a, place * cap, own, own_other)
    place_halves(cot_a, (1 - place) * cap, *near)
    place_halves(cot_b, place * cap, *far)
    place_halves(cot_b, (1 - place) * cap, *farther)
    picks = own_rows(width, n_dp)
    own_a = dot_bt(picks, cot_a[...]).astype(BF16)
    own_b = dot_bt(picks, cot_b[...]).astype(BF16)
    value = dot(own_a, act_a[...]) + dot(own_b, act_b[...])
    write_pieces(value, DOWN_SIDES, pieces)


def last_grad_kernel(
    branch_a, branch_b, att_a, att_b, normed_a, normed_b, proj_a, proj_b,
    sums, sums_other, hidden_sums, *pieces,
):
    parts = [dot(normed_a[...], proj_a[c]) + dot(normed_b[...], proj_b[c]) for c in range(3)]
    parts.append(dot(branch_a[...], att_a[...]) + dot(branch_b[...], att_b[...]))
    value = jnp.concatenate(parts, 1)
    total = sums[...]
    rows = lax.broadcasted_iota(jnp.int32, total.shape, 0)
    total = total + jnp.where(rows < 2, sums_other[...], 0.0)
    bias = hidden_sums[0:1, :] + hidden_sums[1:2, :]
    width = total.shape[1]
    bias = jnp.concatenate([bias[:, :width], bias[:, width:], jnp.zeros((6, width), F32)], 0)
    write_pieces(value, OVER_BOTH, pieces[:-2])
    pieces[-2][...] = total
    pieces[-1][...] = bias
    if len(pieces) > 3:
        for out, small in ((pieces[2], total), (pieces[5], bias)):
            at = out.shape[0] - 8
            out[at : at + 8, :] = small


def middle_kernel(*refs):
    count = len(refs) // 3
    for middle, got, out in zip(refs[:count], refs[count : 2 * count], refs[2 * count :]):
        rows = middle.shape[0]
        out[...] = middle[...] + got[rows : 2 * rows, :]


def last_middle_kernel(middle_x, middle_y, got_x, got_y, small_x, small_y, out_x, out_y):
    rows = middle_x.shape[0]
    for middle, got, small, out in (
        (middle_x, got_x, small_x, out_x),
        (middle_y, got_y, small_y, out_y),
    ):
        out[0:rows, :] = middle[...] + got[rows : 2 * rows, :]
        out[rows : rows + 8, :] = small[...] + got[2 * rows : 2 * rows + 8, :]


def sum_kernel(*refs):
    count = len(refs) // 4
    for i in range(count):
        stay, got, end, out = [refs[k * count + i] for k in range(4)]
        out[...] = (stay[...] + got[0 : stay.shape[0], :]) + end[...]


def write_small(total, bias, qv_bias, gain1, shift1, out_bias, gain2, shift2, up_bias, down_bias):
    width = total.shape[1]
    half = width // 2
    for row, out in enumerate((gain1, shift1, out_bias, gain2, shift2, down_bias)):
        out[...] = total[row]
    qv_bias[0:1, :] = total[6:7, 0:half]
    qv_bias[1:2, :] = total[6:7, half:]
    up_bias[0:width] = bias[0]
    up_bias[width:] = bias[1]


def last_sum_kernel(
    stay_x, stay_y, got_x, got_y, small_x, small_y, end_x, end_y, qkv, out_weight, *outs
):
    rows, half = stay_x.shape
    local = half // 2
    value_x = (stay_x[...] + got_x[0:rows, :]) + end_x[0:rows, :]
    value_y = (stay_y[...] + got_y[0:rows, :]) + end_y[0:rows, :]
    qkv[0] = value_x[:, 0:local]
    qkv[1] = value_x[:, local:]
    qkv[2] = value_y[:, 0:local]
    out_weight[...] = value_y[:, local:]
    total = (small_x[...] + got_x[2 * rows : 2 * rows + 8, :]) + end_x[rows : rows + 8, :]
    bias = (small_y[...] + got_y[2 * rows : 2 * rows + 8, :]) + end_y[rows : rows + 8, :]
    write_small(total, bias, *outs)


def small_kernel(total, bias, *outs):
    write_small(total[...], bias[...], *outs)


def own_slots(n_dp, cap):
    return pl.ds(pl.multiple_of(chunk_place(n_dp) * cap, cap), cap)


def own_pair_kernel(n_dp, grad_normed, act, down, out):
    cap = grad_normed.shape[0]
    out[0:cap, :] = grad_normed[...]
    out[cap:, :] = dot(act[own_slots(n_dp, cap), :], down[...])


def own_block_kernel(
    n_dp, x, gain, grad_after, mine, other, after, down_bias, grad_tokens, layer_out
):
    cap = grad_tokens.shape[0]
    slots = own_slots(n_dp, cap)
    normal, scale = normalize(x[slots, :])
    grad = (mine[0:cap, :] + other[0:cap, :]) * gain[...][None, :]
    grad_tokens[...] = (grad_after[...] + normalize_back(grad, normal, scale)).astype(BF16)
    total = after[slots, :] + (mine[cap:, :] + other[cap:, :])
    layer_out[...] = (total + down_bias[...][None, :]).astype(BF16)


MICROSECONDS = {
    "token_message": 1.5,
    "load": 1.0,
    "load_up": 0.05,
    "copy_tokens": COPY1,
    "cots": COPY2,
    "cot_message": 1.0,
    "attend": ATT,
    "mlp_forward": MLPF,
    "down_grad": 0.1,
    "mlp_back": BACK,
    "up_grad": BACK,
    "attend_back": ATTB,
    "middle": 0.1,
    "middle_up": MIDU,
    "own_pair": 0.1,
    "own_block": 0.1,
    "last_grad": 0.1,
    "sum": 0.1,
    "last_sum": 0.1,
    "small": 0.1,
}


class Sequence:
    def __init__(self):
        self.last = None

    def __call__(
        self, kernel, outs, *args, hbm=(), loose=(), scratch=(), vmem=VMEM_BYTES, name=None, tick=False
    ):
        whole = pl.BlockSpec(memory_space=pltpu.VMEM)

        def place(i):
            if i in hbm:
                return pl.BlockSpec(memory_space=pltpu.HBM)
            return pl.BlockSpec(memory_space=pl.ANY) if i in loose else whole

        specs = [place(i) for i in range(len(args))]
        count = len(args)
        if self.last is not None:
            args = (*args, self.last)
            specs.append(pl.BlockSpec(memory_space=pl.ANY))
        outs = list(outs)
        results_at = len(args) + len(outs)
        if tick:
            outs.append(jax.ShapeDtypeStruct((8, PAIR), F32))

        def run(*refs):
            if tick:
                refs[results_at][...] = jnp.zeros((8, PAIR), F32)
            after = results_at + 1 if tick else results_at
            kernel(*refs[:count], *refs[len(args) : results_at], *refs[after:])

        moved = int(SCALE * MICROSECONDS[name] * 3.5e6)
        results = pl.pallas_call(
            run,
            out_shape=list(outs),
            in_specs=specs,
            out_specs=[whole] * len(outs),
            scratch_shapes=list(scratch),
            compiler_params=pltpu.CompilerParams(vmem_limit_bytes=vmem),
            cost_estimate=pl.CostEstimate(flops=int(moved * 329), bytes_accessed=moved, transcendentals=0),
            name=name,
        )(*args)
        self.last = min(results, key=lambda r: r.size * r.dtype.itemsize)
        return results[:-1] if tick else results


def shape(dims, kind=F32):
    return jax.ShapeDtypeStruct(dims, kind)


def body(
    n_dp, tokens, gain_first, shift_first, qkv_weight, qv_bias, out_weight, out_bias,
    gain_second, shift_second, up_weight, up_bias, down_weight, down_bias, doc_lengths, upstream,
):
    call = Sequence()
    cap, width = tokens.shape
    half = cap // 2
    parts = n_dp // GROUP
    local = qkv_weight.shape[2]
    hidden = up_weight.shape[1]
    share = width // GROUP
    chunk = 2 * cap
    pairs = local // PAIR
    qkv = jnp.transpose(qkv_weight, (1, 0, 2))

    def along(value, k):
        return lax.ppermute(
            value, "dp", [(d, ((d // parts) ^ k) * parts + d % parts) for d in range(n_dp)]
        )

    def across(value, k):
        return lax.ppermute(value, "dp", [(d, d ^ k) for d in range(n_dp)])

    def swap(value):
        return lax.ppermute(value, "tensor", [(0, 1), (1, 0)])

    lanes = (width // PAIR * half, PAIR)
    message, rest, zeros = call(
        token_message_kernel,
        [shape((lanes[0] + 8, PAIR)), shape(lanes), shape((8, width))],
        tokens, doc_lengths, hbm=(0, 1),
        scratch=[
            pltpu.VMEM((cap, width), BF16),
            pltpu.SMEM((SLOTS,), jnp.int32),
            pltpu.SemaphoreType.DMA((2,)),
        ],
        vmem=TOKEN_VMEM, name="token_message",
    )
    near = along(message, 1)
    far = along(message, 2)
    weights = (qkv, out_weight, gain_first, shift_first, qv_bias, rest, zeros)
    qkv, out_weight, gain_first, shift_first, qv_bias, rest, zeros = call(
        load_kernel,
        [shape(a.shape, a.dtype) for a in weights],
        *weights, hbm=tuple(range(len(weights))),
        scratch=[pltpu.SemaphoreType.DMA((len(weights),))],
        name="load",
    )

    def attend(*sources):
        return call(
            functools.partial(attend_kernel, n_dp),
            [
                shape((chunk, width)),
                shape((share, chunk), BF16),
                shape((3, chunk, local), BF16),
                shape((2 * pairs, 2 * cap, cap)),
                shape((chunk, local), BF16),
                shape((chunk, width)),
            ],
            *sources, gain_first, shift_first, qkv, qv_bias, out_weight, name="attend",
        )

    def mlp_forward(x, mine, other):
        return call(
            functools.partial(mlp_forward_kernel, n_dp),
            [
                shape((chunk, width)),
                shape((share, chunk), BF16),
                shape((chunk, hidden), BF16),
                shape((chunk, hidden)),
            ],
            x, mine, other, out_bias, gain_second, shift_second, up_weight, up_bias,
            name="mlp_forward",
        )

    def attend_back(keep_own, *sources):
        return call(
            functools.partial(attend_back_kernel, n_dp, keep_own),
            [
                shape((share, chunk), BF16), shape((3, chunk, local), BF16), shape((8, width)),
                *([shape((cap, width))] * 2 if keep_own else ()),
            ],
            *sources,
            scratch=[pltpu.VMEM((chunk, width), F32)] * 2 if keep_own else (),
            name="attend_back",
        )

    farther = along(far, 1)
    cot_message, cot_rest = call(
        cot_message_kernel,
        [shape((half, width)), shape((half, width))],
        upstream, message, far, loose=(2,),
        scratch=[pltpu.VMEM((cap, width), F32)],
        name="cot_message",
    )
    cot_far = along(cot_message, 2)
    cot_near = along(cot_message, 1)
    cot_farther = along(cot_far, 1)
    weights = (
        up_weight, down_weight, out_bias, gain_second, shift_second, up_bias, down_bias
    )
    up_weight, down_weight, out_bias, gain_second, shift_second, up_bias, down_bias = call(
        load_kernel,
        [shape(a.shape, a.dtype) for a in weights],
        *weights, hbm=tuple(range(len(weights))),
        scratch=[pltpu.SemaphoreType.DMA((len(weights),))],
        name="load_up",
    )
    near_swap, far_swap = swap(near), swap(far)
    (farther,) = call(copy_kernel, [shape(farther.shape)], farther, name="copy_tokens")
    farther_swap = swap(farther)
    x_a, normed_a, proj_a, probs_a, att_a, part_a = attend(message, rest, near, near_swap)
    part_a_other = swap(part_a)
    x_b, normed_b, proj_b, probs_b, att_b, part_b = attend(
        far, far_swap, farther, farther_swap
    )
    part_b_other = swap(part_b)
    (cots,) = call(
        cots_kernel, [shape((3 * half, width))], cot_near, cot_far, cot_farther, name="cots"
    )
    cots_swap = swap(cots)
    after_a, in_a, act_a, slope_a = mlp_forward(x_a, part_a, part_a_other)
    after_b, in_b, act_b, slope_b = mlp_forward(x_b, part_b, part_b_other)

    direct = parts == 4
    count = parts if direct else 1
    piece = share // count
    groups = [[g * parts + r for r in range(parts)] for g in range(GROUP)]

    def piece_shapes(columns, sides, extra=0):
        if not direct:
            return [shape((share, columns))]
        part = columns // len(sides)
        return len(sides) * [
            shape((piece, part)), shape((piece, part)), shape((2 * piece + extra, part))
        ]

    def first_stage(pieces, sides):
        if not direct:
            return ()
        return tuple(across(pieces[3 * i + 2], send) for i, (send, _) in enumerate(sides))

    def scatter(pieces):
        return lax.psum_scatter(
            pieces[0], "dp", scatter_dimension=0, axis_index_groups=groups, tiled=True
        )

    cot_a, cot_b, *down_pieces = call(
        functools.partial(down_grad_kernel, n_dp),
        [shape((chunk, width), BF16), shape((chunk, width), BF16)]
        + piece_shapes(hidden, DOWN_SIDES),
        cot_message, cot_rest, cots, cots_swap,
        act_a, act_b,
        name="down_grad",
    )
    down_got = first_stage(down_pieces, DOWN_SIDES)
    grad_hid_a, grad_hid_b, gm_a, gm_b, bias = call(
        mlp_back_kernel,
        [
            shape((chunk, hidden), BF16), shape((chunk, hidden), BF16),
            shape((chunk, width)), shape((chunk, width)), shape((2, hidden)),
        ],
        cot_a, cot_b, slope_a, slope_b, down_weight, up_weight, name="mlp_back",
    )
    gm_a_other, gm_b_other = swap(gm_a), swap(gm_b)
    up_pieces = call(
        weight_grad_kernel, piece_shapes(hidden, UP_SIDES), in_a, in_b, grad_hid_a, grad_hid_b,
        name="up_grad",
    )
    up_got = first_stage(up_pieces, UP_SIDES)
    branch_a, gp_a, sums_a, grad_after_own, gn_own = attend_back(
        True, gm_a, gm_a_other, after_a, cot_a, gain_second, x_a, gain_first, out_weight, qkv,
        proj_a, probs_a, zeros,
    )
    (own,) = call(
        functools.partial(own_pair_kernel, n_dp), [shape((2 * cap, width))],
        gn_own, act_a, down_weight, name="own_pair",
    )
    own_swap = swap(own)
    branch_b, gp_b, sums = attend_back(
        False, gm_b, gm_b_other, after_b, cot_b, gain_second, x_b, gain_first, out_weight, qkv,
        proj_b, probs_b, sums_a,
    )
    sums_other = swap(sums)
    *last_pieces, total, bias = call(
        last_grad_kernel,
        piece_shapes(4 * local, OVER_BOTH, 8) + [shape((8, width)), shape((8, width))],
        branch_a, branch_b, att_a, att_b, normed_a, normed_b, gp_a, gp_b,
        sums, sums_other, bias,
        name="last_grad",
    )
    last_got = first_stage(last_pieces, OVER_BOTH)
    if direct:
        down_next, up_next = call(
            middle_kernel,
            [shape(down_pieces[1].shape), shape(up_pieces[1].shape)],
            down_pieces[1], up_pieces[1], *down_got, *up_got, name="middle_up",
        )
        down_end, up_end = across(down_next, OVER_X[0][1]), across(up_next, OVER_Y[0][1])
    grad_tokens, layer_out = call(
        functools.partial(own_block_kernel, n_dp),
        [shape((cap, width), BF16), shape((cap, width), BF16)],
        x_a, gain_first, grad_after_own, own, own_swap, after_a, down_bias,
        tick=True, name="own_block",
    )
    if direct:
        stay_x, middle_x, _, stay_y, middle_y, _ = last_pieces
        next_x, next_y = call(
            last_middle_kernel,
            2 * [shape((piece + 8, stay_x.shape[1]))],
            middle_x, middle_y, *last_got, total, bias, name="middle",
        )
        last_got = (
            stay_x, stay_y, *last_got, total, bias, across(next_x, 2), across(next_y, 1)
        )
    else:
        last = scatter(last_pieces)
    if direct:
        grad_down, grad_up = call(
            sum_kernel, [shape((piece, hidden)), shape((piece, hidden))],
            down_pieces[0], up_pieces[0], *down_got, *up_got, down_end, up_end,
            tick=True, name="sum",
        )
    else:
        grad_down, grad_up = scatter(down_pieces), scatter(up_pieces)
    rows = width // n_dp
    small_shapes = [
        shape((2, local)), *([shape((width,))] * 5), shape((hidden,)), shape((width,))
    ]
    if direct:
        grad_qkv, grad_out, *small = call(
            last_sum_kernel,
            [shape((3, rows, local)), shape((rows, local)), *small_shapes],
            *last_got, name="last_sum",
        )
    else:
        grad_qkv = jnp.transpose(last[:, 0 : 3 * local].reshape(rows, 3, local), (1, 0, 2))
        grad_out = last[:, 3 * local :]
        total, bias = lax.psum((total, bias), "dp", axis_index_groups=groups)
        small = call(small_kernel, small_shapes, total, bias, name="small")
    grad_qv, gain1, shift1, grad_out_bias, gain2, shift2, grad_up_bias, grad_down_bias = small
    return (
        layer_out,
        grad_tokens,
        gain1,
        shift1,
        jnp.transpose(grad_qkv, (1, 0, 2)),
        grad_qv,
        grad_out.T,
        grad_out_bias,
        gain2,
        shift2,
        grad_up,
        grad_up_bias,
        grad_down.T,
        grad_down_bias,
    )


def solution(mesh):
    in_specs = (
        P("dp", None),
        P(),
        P(),
        P(None, None, "tensor"),
        P(None, "tensor"),
        P("tensor", None),
        P(),
        P(),
        P(),
        P(None, "tensor"),
        P("tensor"),
        P("tensor", None),
        P(),
        P("dp"),
        P("dp", None),
    )
    out_specs = (
        P("dp", None),
        P("dp", None),
        P(),
        P(),
        P("dp", None, "tensor"),
        P(None, "tensor"),
        P("tensor", "dp"),
        P(),
        P(),
        P(),
        P("dp", "tensor"),
        P("tensor"),
        P("tensor", "dp"),
        P(),
    )
    return jax.shard_map(
        functools.partial(body, mesh.shape["dp"]),
        mesh=mesh,
        in_specs=in_specs,
        out_specs=out_specs,
        check_vma=False,
    )
```

```python
import functools

import jax
import jax.numpy as jnp
from jax import lax
from jax.experimental import pallas as pl
from jax.experimental.pallas import tpu as pltpu
from jax.sharding import PartitionSpec as P

HD = 64
PAIR = 128
GROUP = 4
SLOTS = 4
EPS = 1e-05
F32 = jnp.float32
BF16 = jnp.bfloat16
SCALE = 1.0
FSTEP = 512
COPY1 = 20.0
COPY2 = 20.0
ATTB = 0.05
MIDU = 20.0
ATT = 2.2
MLPF = 1.8
BACK = 0.05
TOKEN_VMEM = 60 * 1024 * 1024
VMEM_BYTES = 16 * 1024 * 1024


def dot(a, b):
    return lax.dot_general(a, b, (((1,), (0,)), ((), ())), preferred_element_type=F32)


def dot_bt(a, b):
    return lax.dot_general(a, b, (((1,), (1,)), ((), ())), preferred_element_type=F32)


def dot_at(a, b):
    return lax.dot_general(a, b, (((0,), (0,)), ((), ())), preferred_element_type=F32)


def normalize(x):
    centred = x - jnp.mean(x, -1, keepdims=True)
    spread = jnp.mean(centred * centred, -1, keepdims=True)
    scale = lax.rsqrt(spread + EPS)
    return centred * scale, scale


def normalize_back(grad, normal, scale):
    return scale * (
        grad
        - jnp.mean(grad, -1, keepdims=True)
        - normal * jnp.mean(grad * normal, -1, keepdims=True)
    )


def own_rows(width, n_dp):
    parts = n_dp // GROUP
    place = lax.axis_index("dp")
    group, rest = place // parts, place % parts
    share = width // GROUP
    if parts != 4:
        row = lax.broadcasted_iota(jnp.int32, (share, width), 0)
        column = lax.broadcasted_iota(jnp.int32, (share, width), 1)
        return (column - row == group * share).astype(F32).astype(BF16)
    piece = share // parts
    row = lax.broadcasted_iota(jnp.int32, (piece, width), 0)
    column = lax.broadcasted_iota(jnp.int32, (piece, width), 1)
    picks = []
    for k in range(parts):
        base = group * share + jnp.bitwise_xor(rest, k) * piece
        picks.append((column - row == base).astype(F32))
    return jnp.concatenate(picks, 0).astype(BF16)


def fetch(pairs, sems):
    copies = [pltpu.make_async_copy(a, b, sems.at[i]) for i, (a, b) in enumerate(pairs)]
    for copy in copies:
        copy.start()
    for copy in copies:
        copy.wait()


def token_message_kernel(
    tokens_hbm, doc_hbm, message, other, zeros, tokens, doc_lengths, sems
):
    fetch(
        [
            (tokens_hbm, tokens),
            (doc_hbm, doc_lengths),
        ],
        sems,
    )
    zeros[...] = jnp.zeros_like(zeros)
    rows, width = tokens.shape
    half = rows // 2
    core = lax.axis_index("tensor")
    here = pl.multiple_of(core * half, half)
    there = pl.multiple_of((1 - core) * half, half)
    for at in range(0, width, PAIR):
        to = at // PAIR * half
        message[to : to + half, :] = tokens[pl.ds(here, half), at : at + PAIR].astype(F32)
        other[to : to + half, :] = tokens[pl.ds(there, half), at : at + PAIR].astype(F32)
    end = jnp.int32(0)
    lines = []
    for j in range(SLOTS):
        end = end + doc_lengths[j]
        lines.append(jnp.full((1, PAIR), end.astype(F32)))
    lines.append(jnp.zeros((8 - SLOTS, PAIR), F32))
    last = width // PAIR * half
    message[last : last + 8, :] = jnp.concatenate(lines, 0)


def cot_message_kernel(upstream, token_message, after, message, other, live):
    rows, width = upstream.shape
    half = rows // 2
    core = lax.axis_index("tensor")
    here = pl.multiple_of(core * half, half)
    there = pl.multiple_of((1 - core) * half, half)
    last = token_message.shape[0] - 8
    end = token_message[last + SLOTS - 1 : last + SLOTS, :]
    slot = lax.broadcasted_iota(jnp.int32, (rows, PAIR), 0).astype(F32)
    filled = slot < end
    for at in range(0, width, PAIR):
        lanes = slice(at, at + PAIR)
        live[:, lanes] = jnp.where(filled, upstream[:, lanes].astype(F32), 0.0)
    message[...] = live[pl.ds(here, half), :]
    other[...] = live[pl.ds(there, half), :]


def cots_kernel(near, far, farther, out):
    half = near.shape[0]
    for i, value in enumerate((near, far, farther)):
        out[i * half : (i + 1) * half, :] = value[...]


def load_kernel(*refs):
    count = (len(refs) - 1) // 2
    fetch(list(zip(refs[:count], refs[count : 2 * count])), refs[-1])


def copy_kernel(value, out):
    out[...] = value[...]


def chunk_place(n_dp):
    return (lax.axis_index("dp") // (n_dp // GROUP)) % 2


def place_halves(target, at, mine, other):
    half = target.shape[0] // 4
    core = lax.axis_index("tensor")
    here = pl.multiple_of(at + core * half, half)
    there = pl.multiple_of(at + (1 - core) * half, half)
    target[pl.ds(here, half), :] = mine[0:half, :].astype(target.dtype)
    target[pl.ds(there, half), :] = other[0:half, :].astype(target.dtype)


def place_tokens(target, at, mine, other):
    half = target.shape[0] // 4
    core = lax.axis_index("tensor")
    here = pl.multiple_of(at + core * half, half)
    there = pl.multiple_of(at + (1 - core) * half, half)
    for lane in range(0, target.shape[1], PAIR):
        start = lane // PAIR * half
        target[pl.ds(here, half), lane : lane + PAIR] = mine[start : start + half, :]
        target[pl.ds(there, half), lane : lane + PAIR] = other[start : start + half, :]


def visible_pairs(ends):
    n = 128
    query = lax.broadcasted_iota(jnp.int32, (n, n), 0).astype(F32)
    key = lax.broadcasted_iota(jnp.int32, (n, n), 1).astype(F32)
    query_segment = jnp.zeros((n, n), F32)
    key_segment = jnp.zeros((n, n), F32)
    for j in range(SLOTS):
        end = ends[j : j + 1, :]
        query_segment += jnp.where(query >= end, 1.0, 0.0)
        key_segment += jnp.where(key >= end, 1.0, 0.0)
    filled = key < ends[SLOTS - 1 : SLOTS, :]
    same = (query_segment == key_segment) & (key <= query) & filled
    return same | (query == key)


def head_masks():
    lane = lax.broadcasted_iota(jnp.int32, (PAIR, PAIR), 1)
    first = lane < HD
    low = jnp.where(first, 1.0, 0.0)
    return first, low.astype(BF16), (1.0 - low).astype(BF16)


def attend_kernel(
    n_dp, mine_a, other_a, mine_b, other_b, gain, shift, qkv, qv_bias, out_weight,
    x_out, own_normed, proj, probs, attended, partial,
):
    cap = 128
    place = chunk_place(n_dp)
    place_tokens(x_out, place * cap, mine_a, other_a)
    place_tokens(x_out, (1 - place) * cap, mine_b, other_b)
    last = mine_a.shape[0] - 8
    ends_a, ends_b = mine_a[last : last + 8, :], mine_b[last : last + 8, :]
    swapped = place == 1
    ends = (jnp.where(swapped, ends_b, ends_a), jnp.where(swapped, ends_a, ends_b))
    x = x_out[...]
    normal, _ = normalize(x)
    normed = (normal * gain[...][None, :] + shift[...][None, :]).astype(BF16)
    for c in range(3):
        value = dot(normed, qkv[c])
        if c == 0:
            value = value + qv_bias[0:1, :]
        if c == 2:
            value = value + qv_bias[1:2, :]
        proj[c] = value.astype(BF16)
    first, low, high = head_masks()
    pairs = attended.shape[1] // PAIR
    places = [
        (block, slice(block * cap, (block + 1) * cap), slice(pair * PAIR, (pair + 1) * PAIR))
        for block in range(2)
        for pair in range(pairs)
    ]
    seen = []
    for block in range(2):
        mask = visible_pairs(ends[block])
        seen.append(jnp.concatenate([mask, mask], 0))
    scores, mixed = [], []
    for block, rows, lanes in places:
        query = proj[0, rows, lanes]
        both = jnp.concatenate([query * low, query * high], 0)
        raw = dot_bt(both, proj[1, rows, lanes]) * (HD**-0.5)
        scores.append(jnp.where(seen[block], raw, -1e30))
    for i, (block, rows, lanes) in enumerate(places):
        weights = jnp.exp(scores[i] - jnp.max(scores[i], -1, keepdims=True))
        prob = weights / jnp.sum(weights, -1, keepdims=True)
        probs[i] = prob
        mixed.append(dot(prob.astype(BF16), proj[2, rows, lanes]))
    for i, (block, rows, lanes) in enumerate(places):
        attended[rows, lanes] = jnp.where(first, mixed[i][0:cap], mixed[i][cap:]).astype(BF16)
    partial[...] = dot(attended[...], out_weight[...])
    own_normed[...] = dot_bt(own_rows(x.shape[1], n_dp), normed).astype(BF16)


def mlp_forward_kernel(
    n_dp, x, mine, other, out_bias, gain, shift, up, up_bias, after, own_in, active, slope
):
    residual = x[...] + (mine[...] + other[...]) + out_bias[...][None, :]
    after[...] = residual
    normal, _ = normalize(residual)
    mlp_in = (normal * gain[...][None, :] + shift[...][None, :]).astype(BF16)
    own_in[...] = dot_bt(own_rows(residual.shape[1], n_dp), mlp_in).astype(BF16)
    step = FSTEP
    c = 0.7978845608028654
    for at in range(0, up.shape[1], step):
        part = slice(at, at + step)
        v = dot(mlp_in, up[:, part]) + up_bias[part][None, :]
        square = v * v
        t = jnp.tanh(v * (c + (0.044715 * c) * square))
        half_more = 0.5 + 0.5 * t
        value = v * half_more
        active[:, part] = value.astype(BF16)
        slope[:, part] = half_more + (value * (1.0 - t)) * (c + (3.0 * 0.044715 * c) * square)


def mlp_back_kernel(
    cot_a, cot_b, slope_a, slope_b, down, up, own_a, own_b,
    partial_a, partial_b, bias_sums, *pieces,
):
    cap = 128
    chunks = ((cot_a, slope_a, own_a, partial_a), (cot_b, slope_b, own_b, partial_b))
    up_grad = []
    for place, (cot, slope, own, partial) in enumerate(chunks):
        low = (dot_bt(cot[...], down[...]) * slope[...]).astype(BF16)
        partial[...] = dot_bt(low, up[...])
        up_grad.append(dot(own[...], low))
        wide = low.astype(F32)
        sums = [
            jnp.sum(wide[block * cap : (block + 1) * cap], 0, keepdims=True) for block in range(2)
        ]
        bias_sums[place : place + 1, :] = sums[0] + sums[1]
    write_pieces(up_grad[0] + up_grad[1], UP_SIDES, pieces)


def attend_back_kernel(
    n_dp, keep_own, mine, other, after, cot, gain2, x, gain1, out_weight, qkv, proj, probs, before,
    own_branch, grad_proj, sums, *own_refs,
):
    cap = 128
    width = x.shape[1]
    normal, scale = normalize(after[...])
    grad_in = mine[...] + other[...]
    live = cot[...].astype(F32)
    grad_after = live + normalize_back(grad_in * gain2[...][None, :], normal, scale)
    branch = grad_after.astype(BF16)
    if keep_own:
        grad_after_own, grad_normed_own, held_after, held_normed = own_refs
        own = pl.ds(pl.multiple_of(chunk_place(n_dp) * cap, cap), cap)
        held_after[...] = grad_after
        grad_after_own[...] = held_after[own, :]
    own_branch[...] = dot_bt(own_rows(width, n_dp), branch).astype(BF16)
    grad_att = dot_bt(branch, out_weight[...]).astype(BF16)
    first, low, high = head_masks()
    pairs = grad_att.shape[1] // PAIR
    places = [
        (slice(block * cap, (block + 1) * cap), slice(pair * PAIR, (pair + 1) * PAIR))
        for block in range(2)
        for pair in range(pairs)
    ]
    both_o, grad_prob, grad_scores = [], [], []
    for rows, lanes in places:
        grad_o = grad_att[rows, lanes]
        both_o.append(jnp.concatenate([grad_o * low, grad_o * high], 0))
        grad_prob.append(dot_bt(both_o[-1], proj[2, rows, lanes]))
    for i in range(len(places)):
        prob = probs[i]
        total = jnp.sum(prob * grad_prob[i], -1, keepdims=True)
        grad_scores.append((prob * (grad_prob[i] - total)).astype(BF16))
    grad_query, grad_key, grad_value = [], [], []
    for i, (rows, lanes) in enumerate(places):
        query = proj[0, rows, lanes]
        both_q = jnp.concatenate([query * low, query * high], 0)
        mixed = dot(grad_scores[i], proj[1, rows, lanes]) * (HD**-0.5)
        grad_query.append(jnp.where(first, mixed[0:cap], mixed[cap:]).astype(BF16))
        grad_key.append((dot_at(grad_scores[i], both_q) * (HD**-0.5)).astype(BF16))
        grad_value.append(dot_at(probs[i].astype(BF16), both_o[i]).astype(BF16))
    for i, (rows, lanes) in enumerate(places):
        grad_proj[0, rows, lanes] = grad_query[i]
        grad_proj[1, rows, lanes] = grad_key[i]
        grad_proj[2, rows, lanes] = grad_value[i]
    grad_normed = (
        dot_bt(grad_proj[0], qkv[0]) + dot_bt(grad_proj[1], qkv[1]) + dot_bt(grad_proj[2], qkv[2])
    )
    if keep_own:
        held_normed[...] = grad_normed
        grad_normed_own[...] = held_normed[own, :]
    normal_first, _ = normalize(x[...])
    here = []
    for block in range(2):
        rows = slice(block * cap, (block + 1) * cap)

        def total(values):
            return jnp.sum(values[rows], 0, keepdims=True)

        here.append(
            jnp.concatenate(
                [
                    total(grad_normed * normal_first),
                    total(grad_normed),
                    total(grad_after),
                    total(grad_in * normal),
                    total(grad_in),
                    total(live),
                    jnp.concatenate(
                        [total(grad_proj[0].astype(F32)), total(grad_proj[2].astype(F32))], 1
                    ),
                    jnp.zeros((1, width), F32),
                ],
                0,
            )
        )
    sums[...] = before[...] + (here[0] + here[1])


OVER_X = ((1, 2),)
OVER_Y = ((2, 1),)
OVER_BOTH = OVER_X + OVER_Y
DOWN_SIDES = OVER_X
UP_SIDES = OVER_Y


def write_pieces(value, sides, pieces):
    if len(pieces) == 1:
        pieces[0][...] = value
        return
    rows = value.shape[0] // 4
    wide = value.shape[1] // len(sides)
    for side, (send, keep) in enumerate(sides):
        stay, middle, out = pieces[3 * side : 3 * side + 3]
        part = value[:, side * wide : (side + 1) * wide]
        stay[...] = part[0:rows]
        middle[...] = part[keep * rows : (keep + 1) * rows]
        out[0:rows, :] = part[send * rows : (send + 1) * rows]
        out[rows : 2 * rows, :] = part[3 * rows : 4 * rows]


def down_grad_kernel(n_dp, *refs):
    own, own_other, cots, cots_other = refs[0:4]
    act_a, act_b, cot_a, cot_b = refs[4:8]
    pieces = refs[8:]
    cap, width = cot_a.shape[0] // 2, cot_a.shape[1]
    place = chunk_place(n_dp)
    half = cap // 2
    near, far, farther = [
        (cots[i * half : (i + 1) * half, :], cots_other[i * half : (i + 1) * half, :])
        for i in range(3)
    ]
    place_halves(cot_a, place * cap, own, own_other)
    place_halves(cot_a, (1 - place) * cap, *near)
    place_halves(cot_b, place * cap, *far)
    place_halves(cot_b, (1 - place) * cap, *farther)
    picks = own_rows(width, n_dp)
    own_a = dot_bt(picks, cot_a[...]).astype(BF16)
    own_b = dot_bt(picks, cot_b[...]).astype(BF16)
    value = dot(own_a, act_a[...]) + dot(own_b, act_b[...])
    write_pieces(value, DOWN_SIDES, pieces)


def last_grad_kernel(
    branch_a, branch_b, att_a, att_b, normed_a, normed_b, proj_a, proj_b,
    sums, sums_other, hidden_sums, *pieces,
):
    parts = [dot(normed_a[...], proj_a[c]) + dot(normed_b[...], proj_b[c]) for c in range(3)]
    parts.append(dot(branch_a[...], att_a[...]) + dot(branch_b[...], att_b[...]))
    value = jnp.concatenate(parts, 1)
    total = sums[...]
    rows = lax.broadcasted_iota(jnp.int32, total.shape, 0)
    total = total + jnp.where(rows < 2, sums_other[...], 0.0)
    bias = hidden_sums[0:1, :] + hidden_sums[1:2, :]
    width = total.shape[1]
    bias = jnp.concatenate([bias[:, :width], bias[:, width:], jnp.zeros((6, width), F32)], 0)
    write_pieces(value, OVER_BOTH, pieces[:-2])
    pieces[-2][...] = total
    pieces[-1][...] = bias
    if len(pieces) > 3:
        for out, small in ((pieces[2], total), (pieces[5], bias)):
            at = out.shape[0] - 8
            out[at : at + 8, :] = small


def middle_kernel(*refs):
    count = len(refs) // 3
    for middle, got, out in zip(refs[:count], refs[count : 2 * count], refs[2 * count :]):
        rows = middle.shape[0]
        out[...] = middle[...] + got[rows : 2 * rows, :]


def last_middle_kernel(middle_x, middle_y, got_x, got_y, small_x, small_y, out_x, out_y):
    rows = middle_x.shape[0]
    for middle, got, small, out in (
        (middle_x, got_x, small_x, out_x),
        (middle_y, got_y, small_y, out_y),
    ):
        out[0:rows, :] = middle[...] + got[rows : 2 * rows, :]
        out[rows : rows + 8, :] = small[...] + got[2 * rows : 2 * rows + 8, :]


def sum_kernel(*refs):
    count = len(refs) // 4
    for i in range(count):
        stay, got, end, out = [refs[k * count + i] for k in range(4)]
        out[...] = (stay[...] + got[0 : stay.shape[0], :]) + end[...]


def write_small(total, bias, qv_bias, gain1, shift1, out_bias, gain2, shift2, up_bias, down_bias):
    width = total.shape[1]
    half = width // 2
    for row, out in enumerate((gain1, shift1, out_bias, gain2, shift2, down_bias)):
        out[...] = total[row]
    qv_bias[0:1, :] = total[6:7, 0:half]
    qv_bias[1:2, :] = total[6:7, half:]
    up_bias[0:width] = bias[0]
    up_bias[width:] = bias[1]


def last_sum_kernel(
    stay_x, stay_y, got_x, got_y, small_x, small_y, end_x, end_y, qkv, out_weight, *outs
):
    rows, half = stay_x.shape
    local = half // 2
    value_x = (stay_x[...] + got_x[0:rows, :]) + end_x[0:rows, :]
    value_y = (stay_y[...] + got_y[0:rows, :]) + end_y[0:rows, :]
    qkv[0] = value_x[:, 0:local]
    qkv[1] = value_x[:, local:]
    qkv[2] = value_y[:, 0:local]
    out_weight[...] = value_y[:, local:]
    total = (small_x[...] + got_x[2 * rows : 2 * rows + 8, :]) + end_x[rows : rows + 8, :]
    bias = (small_y[...] + got_y[2 * rows : 2 * rows + 8, :]) + end_y[rows : rows + 8, :]
    write_small(total, bias, *outs)


def small_kernel(total, bias, *outs):
    write_small(total[...], bias[...], *outs)


def own_slots(n_dp, cap):
    return pl.ds(pl.multiple_of(chunk_place(n_dp) * cap, cap), cap)


def own_pair_kernel(n_dp, grad_normed, act, down, out):
    cap = grad_normed.shape[0]
    out[0:cap, :] = grad_normed[...]
    out[cap:, :] = dot(act[own_slots(n_dp, cap), :], down[...])


def own_block_kernel(
    n_dp, x, gain, grad_after, mine, other, after, down_bias, grad_tokens, layer_out
):
    cap = grad_tokens.shape[0]
    slots = own_slots(n_dp, cap)
    normal, scale = normalize(x[slots, :])
    grad = (mine[0:cap, :] + other[0:cap, :]) * gain[...][None, :]
    grad_tokens[...] = (grad_after[...] + normalize_back(grad, normal, scale)).astype(BF16)
    total = after[slots, :] + (mine[cap:, :] + other[cap:, :])
    layer_out[...] = (total + down_bias[...][None, :]).astype(BF16)


MICROSECONDS = {
    "token_message": 1.5,
    "load": 1.0,
    "load_up": 0.05,
    "copy_tokens": COPY1,
    "cots": COPY2,
    "cot_message": 1.0,
    "attend": ATT,
    "mlp_forward": MLPF,
    "down_grad": 0.1,
    "mlp_back": BACK,
    "attend_back": ATTB,
    "middle": 0.1,
    "middle_up": MIDU,
    "own_pair": 0.1,
    "own_block": 0.1,
    "last_grad": 0.1,
    "sum": 0.1,
    "last_sum": 0.1,
    "small": 0.1,
}


class Sequence:
    def __init__(self):
        self.last = None

    def __call__(
        self, kernel, outs, *args, hbm=(), loose=(), scratch=(), vmem=VMEM_BYTES, name=None, tick=False
    ):
        whole = pl.BlockSpec(memory_space=pltpu.VMEM)

        def place(i):
            if i in hbm:
                return pl.BlockSpec(memory_space=pltpu.HBM)
            return pl.BlockSpec(memory_space=pl.ANY) if i in loose else whole

        specs = [place(i) for i in range(len(args))]
        count = len(args)
        if self.last is not None:
            args = (*args, self.last)
            specs.append(pl.BlockSpec(memory_space=pl.ANY))
        outs = list(outs)
        results_at = len(args) + len(outs)
        if tick:
            outs.append(jax.ShapeDtypeStruct((8, PAIR), F32))

        def run(*refs):
            if tick:
                refs[results_at][...] = jnp.zeros((8, PAIR), F32)
            after = results_at + 1 if tick else results_at
            kernel(*refs[:count], *refs[len(args) : results_at], *refs[after:])

        moved = int(SCALE * MICROSECONDS[name] * 3.5e6)
        results = pl.pallas_call(
            run,
            out_shape=list(outs),
            in_specs=specs,
            out_specs=[whole] * len(outs),
            scratch_shapes=list(scratch),
            compiler_params=pltpu.CompilerParams(vmem_limit_bytes=vmem),
            cost_estimate=pl.CostEstimate(flops=int(moved * 329), bytes_accessed=moved, transcendentals=0),
            name=name,
        )(*args)
        self.last = min(results, key=lambda r: r.size * r.dtype.itemsize)
        return results[:-1] if tick else results


def shape(dims, kind=F32):
    return jax.ShapeDtypeStruct(dims, kind)


def body(
    n_dp, tokens, gain_first, shift_first, qkv_weight, qv_bias, out_weight, out_bias,
    gain_second, shift_second, up_weight, up_bias, down_weight, down_bias, doc_lengths, upstream,
):
    call = Sequence()
    cap, width = tokens.shape
    half = cap // 2
    parts = n_dp // GROUP
    local = qkv_weight.shape[2]
    hidden = up_weight.shape[1]
    share = width // GROUP
    chunk = 2 * cap
    pairs = local // PAIR
    qkv = jnp.transpose(qkv_weight, (1, 0, 2))

    def along(value, k):
        return lax.ppermute(
            value, "dp", [(d, ((d // parts) ^ k) * parts + d % parts) for d in range(n_dp)]
        )

    def across(value, k):
        return lax.ppermute(value, "dp", [(d, d ^ k) for d in range(n_dp)])

    def swap(value):
        return lax.ppermute(value, "tensor", [(0, 1), (1, 0)])

    lanes = (width // PAIR * half, PAIR)
    message, rest, zeros = call(
        token_message_kernel,
        [shape((lanes[0] + 8, PAIR)), shape(lanes), shape((8, width))],
        tokens, doc_lengths, hbm=(0, 1),
        scratch=[
            pltpu.VMEM((cap, width), BF16),
            pltpu.SMEM((SLOTS,), jnp.int32),
            pltpu.SemaphoreType.DMA((2,)),
        ],
        vmem=TOKEN_VMEM, name="token_message",
    )
    near = along(message, 1)
    far = along(message, 2)
    weights = (qkv, out_weight, gain_first, shift_first, qv_bias, rest, zeros)
    qkv, out_weight, gain_first, shift_first, qv_bias, rest, zeros = call(
        load_kernel,
        [shape(a.shape, a.dtype) for a in weights],
        *weights, hbm=tuple(range(len(weights))),
        scratch=[pltpu.SemaphoreType.DMA((len(weights),))],
        name="load",
    )

    def attend(*sources):
        return call(
            functools.partial(attend_kernel, n_dp),
            [
                shape((chunk, width)),
                shape((share, chunk), BF16),
                shape((3, chunk, local), BF16),
                shape((2 * pairs, 2 * cap, cap)),
                shape((chunk, local), BF16),
                shape((chunk, width)),
            ],
            *sources, gain_first, shift_first, qkv, qv_bias, out_weight, name="attend",
        )

    def mlp_forward(x, mine, other):
        return call(
            functools.partial(mlp_forward_kernel, n_dp),
            [
                shape((chunk, width)),
                shape((share, chunk), BF16),
                shape((chunk, hidden), BF16),
                shape((chunk, hidden)),
            ],
            x, mine, other, out_bias, gain_second, shift_second, up_weight, up_bias,
            name="mlp_forward",
        )

    def attend_back(keep_own, *sources):
        return call(
            functools.partial(attend_back_kernel, n_dp, keep_own),
            [
                shape((share, chunk), BF16), shape((3, chunk, local), BF16), shape((8, width)),
                *([shape((cap, width))] * 2 if keep_own else ()),
            ],
            *sources,
            scratch=[pltpu.VMEM((chunk, width), F32)] * 2 if keep_own else (),
            name="attend_back",
        )

    farther = along(far, 1)
    cot_message, cot_rest = call(
        cot_message_kernel,
        [shape((half, width)), shape((half, width))],
        upstream, message, far, loose=(2,),
        scratch=[pltpu.VMEM((cap, width), F32)],
        name="cot_message",
    )
    cot_far = along(cot_message, 2)
    cot_near = along(cot_message, 1)
    cot_farther = along(cot_far, 1)
    weights = (
        up_weight, down_weight, out_bias, gain_second, shift_second, up_bias, down_bias
    )
    up_weight, down_weight, out_bias, gain_second, shift_second, up_bias, down_bias = call(
        load_kernel,
        [shape(a.shape, a.dtype) for a in weights],
        *weights, hbm=tuple(range(len(weights))),
        scratch=[pltpu.SemaphoreType.DMA((len(weights),))],
        name="load_up",
    )
    near_swap, far_swap = swap(near), swap(far)
    (farther,) = call(copy_kernel, [shape(farther.shape)], farther, name="copy_tokens")
    farther_swap = swap(farther)
    x_a, normed_a, proj_a, probs_a, att_a, part_a = attend(message, rest, near, near_swap)
    part_a_other = swap(part_a)
    x_b, normed_b, proj_b, probs_b, att_b, part_b = attend(
        far, far_swap, farther, farther_swap
    )
    part_b_other = swap(part_b)
    (cots,) = call(
        cots_kernel, [shape((3 * half, width))], cot_near, cot_far, cot_farther, name="cots"
    )
    cots_swap = swap(cots)
    after_a, in_a, act_a, slope_a = mlp_forward(x_a, part_a, part_a_other)
    after_b, in_b, act_b, slope_b = mlp_forward(x_b, part_b, part_b_other)

    direct = parts == 4
    count = parts if direct else 1
    piece = share // count
    groups = [[g * parts + r for r in range(parts)] for g in range(GROUP)]

    def piece_shapes(columns, sides, extra=0):
        if not direct:
            return [shape((share, columns))]
        part = columns // len(sides)
        return len(sides) * [
            shape((piece, part)), shape((piece, part)), shape((2 * piece + extra, part))
        ]

    def first_stage(pieces, sides):
        if not direct:
            return ()
        return tuple(across(pieces[3 * i + 2], send) for i, (send, _) in enumerate(sides))

    def scatter(pieces):
        return lax.psum_scatter(
            pieces[0], "dp", scatter_dimension=0, axis_index_groups=groups, tiled=True
        )

    cot_a, cot_b, *down_pieces = call(
        functools.partial(down_grad_kernel, n_dp),
        [shape((chunk, width), BF16), shape((chunk, width), BF16)]
        + piece_shapes(hidden, DOWN_SIDES),
        cot_message, cot_rest, cots, cots_swap,
        act_a, act_b,
        name="down_grad",
    )
    down_got = first_stage(down_pieces, DOWN_SIDES)
    gm_a, gm_b, bias, *up_pieces = call(
        mlp_back_kernel,
        [shape((chunk, width)), shape((chunk, width)), shape((2, hidden))]
        + piece_shapes(hidden, UP_SIDES),
        cot_a, cot_b, slope_a, slope_b, down_weight, up_weight, in_a, in_b, name="mlp_back",
    )
    gm_a_other, gm_b_other = swap(gm_a), swap(gm_b)
    up_got = first_stage(up_pieces, UP_SIDES)
    branch_a, gp_a, sums_a, grad_after_own, gn_own = attend_back(
        True, gm_a, gm_a_other, after_a, cot_a, gain_second, x_a, gain_first, out_weight, qkv,
        proj_a, probs_a, zeros,
    )
    (own,) = call(
        functools.partial(own_pair_kernel, n_dp), [shape((2 * cap, width))],
        gn_own, act_a, down_weight, name="own_pair",
    )
    own_swap = swap(own)
    branch_b, gp_b, sums = attend_back(
        False, gm_b, gm_b_other, after_b, cot_b, gain_second, x_b, gain_first, out_weight, qkv,
        proj_b, probs_b, sums_a,
    )
    sums_other = swap(sums)
    *last_pieces, total, bias = call(
        last_grad_kernel,
        piece_shapes(4 * local, OVER_BOTH, 8) + [shape((8, width)), shape((8, width))],
        branch_a, branch_b, att_a, att_b, normed_a, normed_b, gp_a, gp_b,
        sums, sums_other, bias,
        name="last_grad",
    )
    last_got = first_stage(last_pieces, OVER_BOTH)
    if direct:
        down_next, up_next = call(
            middle_kernel,
            [shape(down_pieces[1].shape), shape(up_pieces[1].shape)],
            down_pieces[1], up_pieces[1], *down_got, *up_got, name="middle_up",
        )
        down_end, up_end = across(down_next, OVER_X[0][1]), across(up_next, OVER_Y[0][1])
    grad_tokens, layer_out = call(
        functools.partial(own_block_kernel, n_dp),
        [shape((cap, width), BF16), shape((cap, width), BF16)],
        x_a, gain_first, grad_after_own, own, own_swap, after_a, down_bias,
        tick=True, name="own_block",
    )
    if direct:
        stay_x, middle_x, _, stay_y, middle_y, _ = last_pieces
        next_x, next_y = call(
            last_middle_kernel,
            2 * [shape((piece + 8, stay_x.shape[1]))],
            middle_x, middle_y, *last_got, total, bias, name="middle",
        )
        last_got = (
            stay_x, stay_y, *last_got, total, bias, across(next_x, 2), across(next_y, 1)
        )
    else:
        last = scatter(last_pieces)
    if direct:
        grad_down, grad_up = call(
            sum_kernel, [shape((piece, hidden)), shape((piece, hidden))],
            down_pieces[0], up_pieces[0], *down_got, *up_got, down_end, up_end,
            tick=True, name="sum",
        )
    else:
        grad_down, grad_up = scatter(down_pieces), scatter(up_pieces)
    rows = width // n_dp
    small_shapes = [
        shape((2, local)), *([shape((width,))] * 5), shape((hidden,)), shape((width,))
    ]
    if direct:
        grad_qkv, grad_out, *small = call(
            last_sum_kernel,
            [shape((3, rows, local)), shape((rows, local)), *small_shapes],
            *last_got, name="last_sum",
        )
    else:
        grad_qkv = jnp.transpose(last[:, 0 : 3 * local].reshape(rows, 3, local), (1, 0, 2))
        grad_out = last[:, 3 * local :]
        total, bias = lax.psum((total, bias), "dp", axis_index_groups=groups)
        small = call(small_kernel, small_shapes, total, bias, name="small")
    grad_qv, gain1, shift1, grad_out_bias, gain2, shift2, grad_up_bias, grad_down_bias = small
    return (
        layer_out,
        grad_tokens,
        gain1,
        shift1,
        jnp.transpose(grad_qkv, (1, 0, 2)),
        grad_qv,
        grad_out.T,
        grad_out_bias,
        gain2,
        shift2,
        grad_up,
        grad_up_bias,
        grad_down.T,
        grad_down_bias,
    )


def solution(mesh):
    in_specs = (
        P("dp", None),
        P(),
        P(),
        P(None, None, "tensor"),
        P(None, "tensor"),
        P("tensor", None),
        P(),
        P(),
        P(),
        P(None, "tensor"),
        P("tensor"),
        P("tensor", None),
        P(),
        P("dp"),
        P("dp", None),
    )
    out_specs = (
        P("dp", None),
        P("dp", None),
        P(),
        P(),
        P("dp", None, "tensor"),
        P(None, "tensor"),
        P("tensor", "dp"),
        P(),
        P(),
        P(),
        P("dp", "tensor"),
        P("tensor"),
        P("tensor", "dp"),
        P(),
    )
    return jax.shard_map(
        functools.partial(body, mesh.shape["dp"]),
        mesh=mesh,
        in_specs=in_specs,
        out_specs=out_specs,
        check_vma=False,
    )
```
